32 devices in a mesh: section: 2 (over core), seq: 4 (over z), head: 4 (over y, x).
Axes of the slice: x: 2, y: 2, z: 4, core: 2. Of those that a mesh axis runs over, the one named last changes fastest.
Arguments:
- section_ends: float32 [2, 2, 4, 4096, 1024], P('section', None, 'seq', 'head'), may hold values from -6 to 6
- norm_gain: float32 [2, 1024], P('section'), may hold values from 0.1 to 1.9
- in_weight: float32 [2, 1024, 4384], P('section', ('seq', 'head')), may hold values from -0.1875 to 0.1875
- conv_weight: float32 [2, 4, 2304], P('section'), may hold values from -3 to 3
- conv_bias: float32 [2, 2304], P('section'), may hold values from -1.2 to 1.2
- dt_bias: float32 [2, 32], P('section'), may hold values from -6 to -2.5
- a_log: float32 [2, 32], P('section'), may hold values from 0 to 2.77
- skip_gain: float32 [2, 32], P('section'), may hold values from 0.5 to 1.5
- gated_gain: float32 [2, 2048], P('section'), may hold values from 0.1 to 1.9
- out_weight: float32 [2, 2048, 1024], P('section', ('seq', 'head')), may hold values from -0.125 to 0.125
Outputs:
- ends_out: float32 [2, 2, 4, 4096, 1024], P('section', None, 'seq', 'head')
- norm_gain_grad: float32 [2, 1024], P('section')
- in_weight_grad: float32 [2, 1024, 4384], P('section', ('seq', 'head'))
- conv_weight_grad: float32 [2, 4, 2304], P('section')
- conv_bias_grad: float32 [2, 2304], P('section')
- dt_bias_grad: float32 [2, 32], P('section')
- a_log_grad: float32 [2, 32], P('section')
- skip_grad: float32 [2, 32], P('section')
- gated_gain_grad: float32 [2, 2048], P('section')
- out_weight_grad: float32 [2, 2048, 1024], P('section', ('seq', 'head'))
The draws below stay inside these ranges and needn't reach their ends.
All inputs are finite; a program needn't handle non-finite values.
Results may differ from the reference program's by a relative error of at most 0.017.
The reference program's roundings to bfloat16 on the way count: a program that leaves them out, or rounds other values in their place, can miss the bound.
Values may be sent and summed in bfloat16 or wider, within the bound.
No kernel may reach another device: no remote copies, remote signals or barrier semaphores. Data moves between devices by JAX's collectives and lax.ppermute only.
A program may use at most 768 MiB of HBM per device.

```python
import jax
import jax.numpy as jnp
from jax import lax

D = 1024
INNER = 2048
HEADS = 32
CONV = 4
BLOCK = 256
LENGTH = 4096
MICRO = 2
SEQS = 4
LAYERS = 2
IN_W = 4384
CONVCH = 2304


def levels(stream_key, shape, cuts, least, largest):
    factor_of, own = 1.0, jax.random.fold_in(stream_key, 6)
    for dim, blocks in cuts:
        heights = jnp.exp(jax.random.uniform(jax.random.fold_in(own, dim), (blocks,), jnp.float32, least / len(cuts), largest / len(cuts)))
        factor_of = factor_of * jnp.repeat(heights, shape[dim] // blocks).reshape([-1 if axis == dim else 1 for axis in range(len(shape))])
    return factor_of


def normal_values(key, shape, spread, reach, shards=(), kind=jnp.bfloat16):
    drawn = spread * jax.random.normal(key, shape, jnp.float32)
    if shards:
        drawn = drawn * levels(key, shape, shards, -0.22, 0.18)
    return jnp.clip(drawn, -reach, reach).astype(kind)


def setup_inputs(seed: int = 0) -> dict:
    arg_keys = jax.random.split(jax.random.key(seed), 11)
    return {
        "section_ends": normal_values(arg_keys[0], (2, MICRO, SEQS, LENGTH, D), 1.0, 6.0, ((0, 2), (2, 4), (3, 4)), jnp.float32),
        "norm_gain": jnp.clip(1.0 + 0.18 * jax.random.normal(arg_keys[1], (LAYERS, D), jnp.float32), 0.1, 1.9),
        "in_weight": normal_values(arg_keys[2], (LAYERS, D, IN_W), D ** -0.5, 0.1875, ((0, 2), (1, 16)), jnp.float32),
        "conv_weight": normal_values(arg_keys[3], (LAYERS, CONV, CONVCH), CONV ** -0.5, 3.0, ((0, 2),), jnp.float32),
        "conv_bias": normal_values(arg_keys[4], (LAYERS, CONVCH), 0.3, 1.2, ((0, 2),), jnp.float32),
        "dt_bias": jnp.clip(-6.0 + 3.5 * jax.random.uniform(arg_keys[5], (LAYERS, HEADS), jnp.float32) ** levels(arg_keys[5], (LAYERS, HEADS), ((0, 2),), -0.2, 0.2), -6.0, -2.5),
        "a_log": jnp.clip(2.77 * jax.random.uniform(arg_keys[6], (LAYERS, HEADS), jnp.float32) ** levels(arg_keys[6], (LAYERS, HEADS), ((0, 2),), -0.2, 0.2), 0.0, 2.77),
        "skip_gain": jnp.clip(0.5 + 1.0 * jax.random.uniform(arg_keys[7], (LAYERS, HEADS), jnp.float32) ** levels(arg_keys[7], (LAYERS, HEADS), ((0, 2),), -0.2, 0.2), 0.5, 1.5),
        "gated_gain": jnp.clip(1.0 + 0.18 * jax.random.normal(arg_keys[8], (LAYERS, INNER), jnp.float32), 0.1, 1.9),
        "out_weight": normal_values(arg_keys[9], (LAYERS, INNER, D), INNER ** -0.5, 0.125, ((0, 2), (1, 16)), jnp.float32),
    }


EPSILON = 1e-05
HIGHEST = lax.Precision.HIGHEST

@jax.custom_vjp
def low(v):
    return lax.optimization_barrier(v.astype(jnp.bfloat16)).astype(jnp.float32)

@jax.custom_vjp
def low_back(v):
    return v

def low_keep(v):
    return (low(v), None)

def low_pass(kept, grad):
    return (grad,)

def back_keep(v):
    return (v, None)

def back_low(kept, grad):
    return (low(grad),)
low.defvjp(low_keep, low_pass)
low_back.defvjp(back_keep, back_low)

def rms_scale(values, gain_vec):
    return values * lax.rsqrt(lax.optimization_barrier(jnp.mean(values * values, axis=-1, keepdims=True)) + EPSILON) * gain_vec

def causal_conv(values, kernel, conv_shift):
    tap_count = kernel.shape[0]
    length = values.shape[0]
    padded = jnp.pad(values, ((tap_count - 1, 0), (0, 0)))
    summed = jnp.zeros_like(values) + conv_shift
    for tap_index in range(tap_count):
        summed = summed + kernel[tap_index] * padded[tap_index:tap_index + length]
    return summed

def block_scan(inputs, step_sizes, decay_rates, b_rows, c_rows):
    length, head_count, head_width = inputs.shape
    blocks = length // BLOCK
    decay_logs = (step_sizes * decay_rates).reshape(blocks, BLOCK, head_count).transpose(0, 2, 1)
    within = jnp.cumsum(decay_logs, axis=2)
    scaled = (inputs * step_sizes[:, :, None]).reshape(blocks, BLOCK, head_count, head_width)
    b_blocks = b_rows.reshape(blocks, BLOCK, -1)
    c_blocks = c_rows.reshape(blocks, BLOCK, -1)
    scores = jnp.einsum('cis,cjs->cij', c_blocks, b_blocks, precision=HIGHEST)
    position = jnp.arange(BLOCK)
    lower_mask = position[:, None] >= position[None, :]
    gap_logs = within[:, :, :, None] - within[:, :, None, :]
    weights_in = jnp.exp(jnp.where(lower_mask, gap_logs, -jnp.inf)) * scores[:, None]
    diagonal = jnp.einsum('chij,cjhp->cihp', weights_in, scaled, precision=HIGHEST)
    ending = within[:, :, -1]
    to_end = jnp.exp(ending[:, :, None] - within)
    states = jnp.einsum('chj,cjs,cjhp->chsp', to_end, b_blocks, scaled, precision=HIGHEST)
    totals = jnp.cumsum(ending, axis=0)
    before = totals - ending
    block_order = jnp.arange(blocks)
    earlier = block_order[:, None] > block_order[None, :]
    carry_links = jnp.exp(jnp.where(earlier[:, :, None], before[:, None, :] - totals[None, :, :], -jnp.inf))
    entering = jnp.einsum('kmh,mhsp->khsp', carry_links, states, precision=HIGHEST)
    offdiag = jnp.einsum('cis,chsp,chi->cihp', c_blocks, entering, jnp.exp(within), precision=HIGHEST)
    return (diagonal + offdiag).reshape(length, head_count, head_width)

def ssm_mixer(x_values, step_values, bc_values, kernel, conv_shift, step_bias, decay_log, skip_vec):
    length = x_values.shape[0]
    channels = x_values.shape[1]
    head_count = step_values.shape[1]
    state_width = bc_values.shape[1] // 2
    convolved = jax.nn.silu(causal_conv(jnp.concatenate([x_values, bc_values], axis=1), kernel, conv_shift))
    inputs = convolved[:, :channels].reshape(length, head_count, channels // head_count)
    b_rows = convolved[:, channels:channels + state_width]
    c_rows = convolved[:, channels + state_width:]
    step_sizes = jax.nn.softplus(step_values + step_bias)
    decay_rates = -jnp.exp(decay_log)
    output = block_scan(inputs, step_sizes, decay_rates, b_rows, c_rows) + skip_vec[:, None] * inputs
    return output.reshape(length, channels)

def mamba_layer(hidden, gain_vec, in_matrix, kernel, conv_shift, step_bias, decay_log, skip_vec, gate_gain, out_matrix):
    inner_width = gate_gain.shape[0]
    state_width = (conv_shift.shape[0] - inner_width) // 2
    x_end = 2 * inner_width
    bc_end = x_end + 2 * state_width
    normed = low(rms_scale(hidden, gain_vec))
    projected = low_back(jnp.dot(normed, low(in_matrix), precision=HIGHEST))
    gate_part = projected[:, :inner_width]
    x_part = low_back(low(projected[:, inner_width:x_end]))
    bc_part = low(projected[:, x_end:bc_end])
    step_part = low_back(low(projected[:, bc_end:]))
    mixed_heads = low_back(low(ssm_mixer(x_part, step_part, bc_part, kernel, conv_shift, step_bias, decay_log, skip_vec)))
    gated_rows = rms_scale(mixed_heads * jax.nn.silu(gate_part), gate_gain)
    branch = low_back(jnp.dot(low(gated_rows), low(out_matrix), precision=HIGHEST))
    return hidden + branch

def reference(section_ends, norm_gain, in_weight, conv_weight, conv_bias, dt_bias, a_log, skip_gain, gated_gain, out_weight):
    params = (norm_gain.astype(jnp.float32), in_weight.astype(jnp.float32), conv_weight.astype(jnp.float32), conv_bias.astype(jnp.float32), dt_bias.astype(jnp.float32), a_log.astype(jnp.float32), skip_gain.astype(jnp.float32), gated_gain.astype(jnp.float32), out_weight.astype(jnp.float32))
    flattened = section_ends.astype(jnp.float32).reshape(2, MICRO * SEQS, LENGTH, D)

    def forward(hidden, weights):
        for layer_index in range(LAYERS):
            hidden = mamba_layer(hidden, *tuple((member[layer_index] for member in weights)))
        return hidden

    def one_sequence(totals, sequence_pair):
        outputs, pullback = jax.vjp(forward, sequence_pair[0], params)
        grad_input, grad_params = pullback(sequence_pair[1])
        totals = jax.tree.map(jnp.add, totals, grad_params)
        return (totals, (outputs, grad_input))
    zeros_init = jax.tree.map(jnp.zeros_like, params)
    totals, (outputs, inputs_grad) = lax.scan(one_sequence, zeros_init, (flattened[0], flattened[1]))
    ends_out = jnp.stack([inputs_grad, outputs]).reshape(2, MICRO, SEQS, LENGTH, D)
    return (ends_out, totals[0], totals[1], totals[2], totals[3], totals[4], totals[5], totals[6], totals[7], totals[8])
```

```python
import functools

import jax
import jax.numpy as jnp
from jax import lax
from jax.experimental import pallas as pl
from jax.experimental.pallas import tpu as pltpu
from jax.sharding import PartitionSpec as P

BLOCK = 256
LANES = 128
EPSILON = 1e-05
LOG2E = 1.4426950408889634
HIGHEST = lax.Precision.HIGHEST
F32 = jnp.float32
LOW = jnp.bfloat16
VMEM_BYTES = 56 * 1024 * 1024


def contract(a, b, a_dim, b_dim, precision=None):
    return lax.dot_general(
        a, b, (((a_dim,), (b_dim,)), ((), ())), preferred_element_type=F32, precision=precision
    )


def sigmoid(v):
    return 0.5 * jnp.tanh(0.5 * v) + 0.5


def softplus(v):
    return jnp.maximum(v, 0.0) + jnp.log1p(jnp.exp(-jnp.abs(v)))


def wide(column):
    return jnp.concatenate([column, column], axis=-1)


def upper_ones():
    row = lax.broadcasted_iota(jnp.int32, (BLOCK, BLOCK), 0)
    col = lax.broadcasted_iota(jnp.int32, (BLOCK, BLOCK), 1)
    return (row <= col).astype(F32)


def lower_ones():
    row = lax.broadcasted_iota(jnp.int32, (BLOCK, BLOCK), 0)
    col = lax.broadcasted_iota(jnp.int32, (BLOCK, BLOCK), 1)
    return (row >= col).astype(F32)


def rolled_taps(u_wide, taps):
    out = []
    for k in range(taps):
        back = taps - 1 - k
        moved = u_wide if back == 0 else pltpu.roll(u_wide, back, 1)
        out.append(moved[:, LANES:])
    return out


def call(kernel, grid, ins, outs, scratch, flops, nbytes, transcendentals=0):
    arrays = [a for a, _ in ins]
    return pl.pallas_call(
        kernel,
        grid=grid,
        in_specs=[s for _, s in ins],
        out_specs=[s for _, s in outs],
        out_shape=[a for a, _ in outs],
        scratch_shapes=scratch,
        compiler_params=pltpu.CompilerParams(
            dimension_semantics=("arbitrary",) * len(grid), vmem_limit_bytes=VMEM_BYTES
        ),
        cost_estimate=pl.CostEstimate(
            flops=flops, bytes_accessed=nbytes, transcendentals=transcendentals
        ),
    )(*arrays)


def whole(array):
    rank = len(array.shape)
    return (
        array, pl.BlockSpec(array.shape, lambda b: (0,) * rank, pipeline_mode=pl.Buffered(1))
    )


def tokens(array):
    return (array, pl.BlockSpec((array.shape[0], BLOCK), lambda b: (0, b)))


def out(shape, dtype):
    return jax.ShapeDtypeStruct(shape, dtype)


def states_kernel(
    u_ref, halo_ref, step_ref, cw_ref, cb_ref, bias_ref, rate_ref,
    xs_ref, bc_ref, dt_ref, w_ref, wt_ref, wcol_ref, sin_ref, send_ref,
    tail, state, xd, scale, ewend, offset,
):
    step = pl.program_id(0)
    heads = step_ref.shape[0]
    inner = xs_ref.shape[0]
    width = inner // heads
    taps = cw_ref.shape[0]
    n_state = bc_ref.shape[0] // 2

    @pl.when(step == 0)
    def _():
        tail[...] = halo_ref[...]
        state[...] = jnp.zeros_like(state)
        offset[...] = jnp.zeros_like(offset)

    dt = softplus(step_ref[...].astype(F32) + bias_ref[...])
    loga = dt * rate_ref[...]
    upper = upper_ones()
    w = contract(loga, upper, 1, 0, HIGHEST)
    wcol_ref[...] = contract(lower_ones(), loga, 1, 1, HIGHEST)
    wend = w[:, BLOCK - 1 :]
    dt_ref[...] = dt
    w_ref[...] = w
    wt_ref[...] = w + offset[:, :1]
    offset[...] += jnp.broadcast_to(wend, offset.shape)
    scale[...] = dt * jnp.exp(wend - w)
    ewend[...] = jnp.broadcast_to(jnp.exp(wend), ewend.shape)

    def conv(rows):
        u = jnp.concatenate([tail[rows, :], u_ref[rows, :]], axis=1).astype(F32)
        c = wide(cb_ref[rows, :])
        for k, moved in enumerate(rolled_taps(u, taps)):
            c = c + wide(cw_ref[k, rows, :]) * moved
        return c * sigmoid(c)

    def head(h, _):
        rows = pl.ds(pl.multiple_of(h * width, width), width)
        xs = conv(rows)
        xs_ref[rows, :] = xs.astype(LOW)
        xd[rows, :] = (xs * scale[pl.ds(h, 1), :]).astype(LOW)
        return 0

    lax.fori_loop(0, heads, head, 0)

    def shared(i, _):
        rows = pl.ds(pl.multiple_of(inner + i * width, width), width)
        own = pl.ds(pl.multiple_of(i * width, width), width)
        bc_ref[own, :] = conv(rows).astype(LOW)
        return 0

    lax.fori_loop(0, 2 * n_state // width, shared, 0)
    tail[...] = u_ref[:, BLOCK - LANES :]
    sin_ref[0] = state[...].astype(LOW)

    def advance(h, _):
        rows = pl.ds(pl.multiple_of(h * width, width), width)
        fresh = contract(xd[rows, :], bc_ref[:n_state, :], 1, 1)
        state[rows, :] = ewend[pl.ds(h, 1), :] * state[rows, :] + fresh
        return 0

    lax.fori_loop(0, heads, advance, 0)

    @pl.when(step == pl.num_programs(0) - 1)
    def _():
        send_ref[:inner, :] = state[...].astype(LOW)
        send_ref[inner:, :] = jnp.exp(offset[...]).astype(LOW)


def scan_states(u, halo, step_low, cw, cb, bias, rate, n_state):
    channels, length = u.shape
    heads = step_low.shape[0]
    inner = channels - 2 * n_state
    blocks = length // BLOCK
    tok = lambda rows, dtype: (
        out((rows, length), dtype), pl.BlockSpec((rows, BLOCK), lambda b: (0, b))
    )
    return call(
        states_kernel,
        (blocks,),
        [tokens(u), whole(halo), tokens(step_low), whole(cw), whole(cb), whole(bias), whole(rate)],
        [
            tok(inner, LOW),
            tok(2 * n_state, LOW),
            tok(heads, F32),
            tok(heads, F32),
            tok(heads, F32),
            (out((length, heads), F32), pl.BlockSpec((BLOCK, heads), lambda b: (b, 0))),
            (
                out((blocks, inner, n_state), LOW),
                pl.BlockSpec((1, inner, n_state), lambda b: (b, 0, 0)),
            ),
            (
                out((inner + heads, n_state), LOW),
                pl.BlockSpec((inner + heads, n_state), lambda b: (0, 0)),
            ),
        ],
        [
            pltpu.VMEM((channels, LANES), LOW),
            pltpu.VMEM((inner, n_state), F32),
            pltpu.VMEM((inner, BLOCK), LOW),
            pltpu.VMEM((heads, BLOCK), F32),
            pltpu.VMEM((heads, LANES), F32),
            pltpu.VMEM((heads, LANES), F32),
        ],
        2 * length * inner * n_state,
        channels * length * 6,
        channels * length,
    )


def spread_columns(wcol_ref, wb):
    for h in range(wb.shape[0]):
        wb[h] = jnp.broadcast_to(wcol_ref[:, h : h + 1] * LOG2E, (BLOCK, LANES))


def masked_scores(bc_ref, n_state):
    scores = contract(bc_ref[:n_state, :], bc_ref[n_state:, :], 0, 0)
    row = lax.broadcasted_iota(jnp.int32, (BLOCK, BLOCK), 0)
    col = lax.broadcasted_iota(jnp.int32, (BLOCK, BLOCK), 1)
    return jnp.where(row <= col, scores, 0.0)


def decay(wrow, wb_h):
    return jnp.exp2(jnp.minimum(wrow * LOG2E - wide(wb_h), 0.0))


def local_kernel(xs_ref, bc_ref, dt_ref, w_ref, wcol_ref, sin_ref, y_ref, wb, scores):
    heads = dt_ref.shape[0]
    inner = xs_ref.shape[0]
    width = inner // heads
    n_state = bc_ref.shape[0] // 2
    spread_columns(wcol_ref, wb)
    scores[...] = masked_scores(bc_ref, n_state)
    y_ref[...] = contract(sin_ref[0], bc_ref[n_state:, :], 1, 0)

    def head(h, _):
        rows = pl.ds(pl.multiple_of(h * width, width), width)
        wrow = w_ref[pl.ds(h, 1), :]
        xdt = (xs_ref[rows, :].astype(F32) * dt_ref[pl.ds(h, 1), :]).astype(LOW)
        weights = (scores[...] * decay(wrow, wb[h])).astype(LOW)
        y_ref[rows, :] = y_ref[rows, :] * jnp.exp(wrow) + contract(xdt, weights, 1, 0)
        return 0

    lax.fori_loop(0, heads, head, 0)


def scan_local(xs, bc, dt, w, wcol, sin):
    inner, length = xs.shape
    heads = dt.shape[0]
    return call(
        local_kernel,
        (length // BLOCK,),
        [
            tokens(xs),
            tokens(bc),
            tokens(dt),
            tokens(w),
            (wcol, pl.BlockSpec((BLOCK, heads), lambda b: (b, 0))),
            (sin, pl.BlockSpec((1,) + sin.shape[1:], lambda b: (b, 0, 0))),
        ],
        [(out((inner, length), F32), pl.BlockSpec((inner, BLOCK), lambda b: (0, b)))],
        [pltpu.VMEM((heads, BLOCK, LANES), F32), pltpu.VMEM((BLOCK, BLOCK), F32)],
        2 * length * inner * (BLOCK * 4 + bc.shape[0] // 2),
        inner * length * 7,
        heads * length * BLOCK,
    )[0]


def gate_kernel(
    yl_ref, xs_ref, z_ref, bc_ref, wt_ref, sdev_ref, skip_ref, gain_ref,
    ylow_ref, gated_ref, corr, v_scr,
):
    inner = yl_ref.shape[0]
    heads = wt_ref.shape[0]
    width = inner // heads
    n_state = bc_ref.shape[0] // 2
    corr[...] = contract(sdev_ref[...], bc_ref[n_state:, :], 1, 0)

    def head(h, total):
        rows = pl.ds(pl.multiple_of(h * width, width), width)
        one = pl.ds(h, 1)
        y = (
            yl_ref[rows, :]
            + jnp.exp(wt_ref[one, :]) * corr[rows, :]
            + skip_ref[one, :] * xs_ref[rows, :].astype(F32)
        ).astype(LOW)
        ylow_ref[rows, :] = y
        z = z_ref[rows, :].astype(F32)
        v = y.astype(F32) * (z * sigmoid(z))
        v_scr[rows, :] = v
        return total + jnp.sum((v * v).reshape(width // 8, 8, BLOCK), axis=0)

    total = lax.fori_loop(0, heads, head, jnp.zeros((8, BLOCK), F32))
    r = lax.rsqrt(jnp.sum(total, axis=0, keepdims=True) / inner + EPSILON)

    def norm(h, _):
        rows = pl.ds(pl.multiple_of(h * width, width), width)
        gated_ref[rows, :] = (v_scr[rows, :] * r * wide(gain_ref[rows, :])).astype(LOW)
        return 0

    lax.fori_loop(0, heads, norm, 0)


def gate_forward(yl, xs, z, bc, wt, sdev, skip, gain):
    inner, length = yl.shape
    tok = lambda dtype: (
        out((inner, length), dtype), pl.BlockSpec((inner, BLOCK), lambda b: (0, b))
    )
    return call(
        gate_kernel,
        (length // BLOCK,),
        [tokens(yl), tokens(xs), tokens(z), tokens(bc), tokens(wt), whole(sdev), whole(skip), whole(gain)],
        [tok(LOW), tok(LOW)],
        [pltpu.VMEM((inner, BLOCK), F32), pltpu.VMEM((inner, BLOCK), F32)],
        2 * length * inner * sdev.shape[1],
        inner * length * 14,
        inner * length,
    )


def gate_back_kernel(
    dg_ref, ylow_ref, z_ref, bc_ref, wt_ref, gain_ref,
    dy_ref, dz_ref, gg_ref, send_ref, dye, ds,
):
    step = pl.program_id(0)
    inner = dg_ref.shape[0]
    heads = wt_ref.shape[0]
    width = inner // heads
    n_state = bc_ref.shape[0] // 2

    @pl.when(step == 0)
    def _():
        gg_ref[...] = jnp.zeros_like(gg_ref)
        ds[...] = jnp.zeros_like(ds)

    def first(h, sums):
        squares, means = sums
        rows = pl.ds(pl.multiple_of(h * width, width), width)
        z = z_ref[rows, :].astype(F32)
        v = ylow_ref[rows, :].astype(F32) * (z * sigmoid(z))
        m = v * (dg_ref[rows, :] * wide(gain_ref[rows, :]))
        fold = lambda a: jnp.sum(a.reshape(width // 8, 8, BLOCK), axis=0)
        return squares + fold(v * v), means + fold(m)

    zero = jnp.zeros((8, BLOCK), F32)
    squares, means = lax.fori_loop(0, heads, first, (zero, zero))
    r = lax.rsqrt(jnp.sum(squares, axis=0, keepdims=True) / inner + EPSILON)
    back = r * r * r * (jnp.sum(means, axis=0, keepdims=True) / inner)

    def second(h, _):
        rows = pl.ds(pl.multiple_of(h * width, width), width)
        z = z_ref[rows, :].astype(F32)
        sig = sigmoid(z)
        silu = z * sig
        y = ylow_ref[rows, :].astype(F32)
        v = y * silu
        du = dg_ref[rows, :]
        dv = r * (wide(gain_ref[rows, :]) * du) - v * back
        dy = (dv * silu).astype(LOW)
        dy_ref[rows, :] = dy
        dz_ref[rows, :] = (dv * y * (sig * (1.0 + z * (1.0 - sig)))).astype(LOW)
        gg = du * v * r
        gg_ref[rows, :] += gg[:, :LANES] + gg[:, LANES:]
        dye[rows, :] = (dy.astype(F32) * jnp.exp(wt_ref[pl.ds(h, 1), :])).astype(LOW)
        return 0

    lax.fori_loop(0, heads, second, 0)
    ds[...] += contract(dye[...], bc_ref[n_state:, :], 1, 1)

    @pl.when(step == pl.num_programs(0) - 1)
    def _():
        send_ref[...] = ds[...].astype(LOW)


def gate_backward(dg, ylow, z, bc, wt, gain):
    inner, length = dg.shape
    n_state = bc.shape[0] // 2
    tok = lambda dtype: (
        out((inner, length), dtype), pl.BlockSpec((inner, BLOCK), lambda b: (0, b))
    )
    fixed = lambda cols, dtype: (
        out((inner, cols), dtype), pl.BlockSpec((inner, cols), lambda b: (0, 0))
    )
    return call(
        gate_back_kernel,
        (length // BLOCK,),
        [tokens(dg), tokens(ylow), tokens(z), tokens(bc), tokens(wt), whole(gain)],
        [tok(LOW), tok(LOW), fixed(LANES, F32), fixed(n_state, LOW)],
        [pltpu.VMEM((inner, BLOCK), LOW), pltpu.VMEM((inner, n_state), F32)],
        2 * length * inner * n_state,
        inner * length * 14,
        2 * inner * length,
    )


def local_back_kernel(
    xs_ref, dy_ref, bc_ref, dt_ref, w_ref, wcol_ref, dx_ref, rows_ref, dbc_ref, wb, scores, dscores
):
    heads = dt_ref.shape[0]
    inner = xs_ref.shape[0]
    width = inner // heads
    n_state = bc_ref.shape[0] // 2
    spread_columns(wcol_ref, wb)
    scores[...] = masked_scores(bc_ref, n_state)
    dscores[...] = jnp.zeros_like(dscores)

    def head(h, _):
        rows = pl.ds(pl.multiple_of(h * width, width), width)
        one = pl.ds(h, 1)
        xdt = (xs_ref[rows, :].astype(F32) * dt_ref[one, :]).astype(LOW)
        dy = dy_ref[rows, :]
        decays = decay(w_ref[one, :], wb[h])
        weights = (scores[...] * decays).astype(LOW)
        y = contract(xdt, weights, 1, 0)
        dx = contract(dy, weights, 1, 1)
        dscores[...] += decays * contract(xdt, dy, 0, 0)
        dx_ref[rows, :] = dx
        rows_ref[one, :] = jnp.sum(
            dy.astype(F32) * y - xdt.astype(F32) * dx, axis=0, keepdims=True
        )
        return 0

    lax.fori_loop(0, heads, head, 0)
    row = lax.broadcasted_iota(jnp.int32, (BLOCK, BLOCK), 0)
    col = lax.broadcasted_iota(jnp.int32, (BLOCK, BLOCK), 1)
    masked = jnp.where(row <= col, dscores[...], 0.0).astype(LOW)
    dbc_ref[:n_state, :] = contract(bc_ref[n_state:, :], masked, 1, 1)
    dbc_ref[n_state:, :] = contract(bc_ref[:n_state, :], masked, 1, 0)


def scan_local_back(xs, dy, bc, dt, w, wcol):
    inner, length = xs.shape
    heads = dt.shape[0]
    tok = lambda rows, dtype: (
        out((rows, length), dtype), pl.BlockSpec((rows, BLOCK), lambda b: (0, b))
    )
    return call(
        local_back_kernel,
        (length // BLOCK,),
        [
            tokens(xs),
            tokens(dy),
            tokens(bc),
            tokens(dt),
            tokens(w),
            (wcol, pl.BlockSpec((BLOCK, heads), lambda b: (b, 0))),
        ],
        [tok(inner, F32), tok(heads, F32), tok(bc.shape[0], F32)],
        [
            pltpu.VMEM((heads, BLOCK, LANES), F32),
            pltpu.VMEM((BLOCK, BLOCK), F32),
            pltpu.VMEM((BLOCK, BLOCK), F32),
        ],
        2 * length * inner * BLOCK * 12,
        inner * length * 8,
        heads * length * BLOCK,
    )


def states_back_kernel(
    u_ref, before_ref, halo_ref, step_ref, xs_ref, dy_ref, dxl_ref, dbcl_ref, bc_ref,
    dt_ref, w_ref, wt_ref, rows_ref, sin_ref, sdev_ref, dsend_ref,
    cw_ref, cb_ref, bias_ref, rate_ref, skip_ref,
    du_ref, dstep_ref, first_ref, last_ref, gconv_ref, ghead_ref,
    ds, dsl, sinl, q, yo, xde, dye, toend, ew, ewend, offs, rr, kk, ddt, ee, right,
):
    step = pl.program_id(0)
    final = pl.num_programs(0) - 1
    heads = step_ref.shape[0]
    inner = xs_ref.shape[0]
    width = inner // heads
    n_state = bc_ref.shape[0] // 2
    taps = cw_ref.shape[0]

    @pl.when(step == 0)
    def _():
        ds[...] = dsend_ref[...]
        right[...] = jnp.zeros_like(right)
        gconv_ref[...] = jnp.zeros_like(gconv_ref)
        ghead_ref[...] = jnp.zeros_like(ghead_ref)

    w = w_ref[...]
    wend = w[:, BLOCK - 1 :]
    toend[...] = jnp.exp(wend - w)
    ew[...] = jnp.exp(w)
    ewend[...] = jnp.broadcast_to(jnp.exp(wend), ewend.shape)
    offs[...] = jnp.exp(wt_ref[:, :LANES] - w[:, :LANES])

    def enter(h, _):
        rows = pl.ds(pl.multiple_of(h * width, width), width)
        one = pl.ds(h, 1)
        entering = sin_ref[0, rows, :].astype(F32) + offs[one, :] * sdev_ref[rows, :].astype(F32)
        d = ds[rows, :]
        ee[one, :] = ewend[one, :] * jnp.sum(d * entering, axis=0, keepdims=True)
        sinl[rows, :] = entering.astype(LOW)
        dsl[rows, :] = d.astype(LOW)
        return 0

    lax.fori_loop(0, heads, enter, 0)
    b_low = bc_ref[:n_state, :]
    c_low = bc_ref[n_state:, :]
    q[...] = contract(dsl[...], b_low, 1, 0)
    yo[...] = contract(sinl[...], c_low, 1, 0)

    def conv_back(rows, dxs):
        before = jnp.where(step == final, halo_ref[rows, :], before_ref[rows, :])
        u = jnp.concatenate([before, u_ref[rows, :]], axis=1).astype(F32)
        moved = rolled_taps(u, taps)
        c = wide(cb_ref[rows, :])
        for k in range(taps):
            c = c + wide(cw_ref[k, rows, :]) * moved[k]
        sig = sigmoid(c)
        dc = dxs * (sig * (1.0 + c * (1.0 - sig)))
        fold = lambda a: a[:, :LANES] + a[:, LANES:]
        for k in range(taps):
            gconv_ref[k, rows, :] += fold(dc * moved[k])
        gconv_ref[taps, rows, :] += fold(dc)
        following = jnp.concatenate([dc, right[rows, :]], axis=1)
        du = wide(cw_ref[taps - 1, rows, :]) * dc
        for k in range(taps - 1):
            ahead = taps - 1 - k
            du = du + wide(cw_ref[k, rows, :]) * (
                pltpu.roll(following, BLOCK + LANES - ahead, 1)[:, :BLOCK]
            )
        du_ref[rows, :] = du.astype(LOW)

        @pl.when(step == 0)
        def _():
            last_ref[rows, :] = du[:, BLOCK - LANES :]

        right[rows, :] = dc[:, :LANES]

    def head(h, _):
        rows = pl.ds(pl.multiple_of(h * width, width), width)
        one = pl.ds(h, 1)
        xs = xs_ref[rows, :].astype(F32)
        dt = dt_ref[one, :]
        te = toend[one, :]
        eh = ew[one, :]
        dy = dy_ref[rows, :].astype(F32)
        xdt = (xs * dt).astype(LOW).astype(F32)
        dx_state = te * q[rows, :]
        kk[one, :] = jnp.sum(xdt * dx_state, axis=0, keepdims=True)
        rr[one, :] = rows_ref[one, :] + jnp.sum(dy * eh * yo[rows, :], axis=0, keepdims=True)
        xde[rows, :] = (xdt * te).astype(LOW)
        dye[rows, :] = (dy * eh).astype(LOW)
        dx = dxl_ref[rows, :] + dx_state
        ddt[one, :] = jnp.sum(dx * xs, axis=0, keepdims=True)
        ghead_ref[2, one, :] += jnp.sum(dy * xs, axis=0, keepdims=True)
        conv_back(rows, dx * dt + skip_ref[one, :] * dy)
        return 0

    lax.fori_loop(0, heads, head, 0)

    db = dbcl_ref[:n_state, :] + contract(dsl[...], xde[...], 0, 0)
    dc = dbcl_ref[n_state:, :] + contract(sinl[...], dye[...], 0, 0)
    conv_back(pl.ds(inner, n_state), db)
    conv_back(pl.ds(inner + n_state, n_state), dc)

    upper = upper_ones()
    dloga = (
        contract(rr[...], upper, 1, 1, HIGHEST)
        + (contract(kk[...], upper, 1, 0, HIGHEST) - kk[...])
        + jnp.sum(ee[...], axis=1, keepdims=True)
    )
    rate = rate_ref[...]
    dt = dt_ref[...]
    raw = step_ref[...].astype(F32) + bias_ref[...]
    dstep = (ddt[...] + dloga * rate) * jax.nn.sigmoid(raw)
    dstep_ref[...] = dstep.astype(LOW)
    ghead_ref[0] += dstep
    ghead_ref[1] += dloga * dt * rate

    def advance(h, _):
        rows = pl.ds(pl.multiple_of(h * width, width), width)
        ds[rows, :] = ewend[pl.ds(h, 1), :] * ds[rows, :] + contract(dye[rows, :], c_low, 1, 1)
        return 0

    lax.fori_loop(0, heads, advance, 0)

    @pl.when(step == final)
    def _():
        first_ref[...] = right[...]


def scan_states_back(
    u, halo, step_low, xs, dy, dx_local, dbc_local, bc, dt, w, wt, row_sums, sin, sdev, dsend,
    cw, cb, bias, rate, skip,
):
    channels, length = u.shape
    heads = dt.shape[0]
    inner = xs.shape[0]
    blocks = length // BLOCK
    n_state = bc.shape[0] // 2
    taps = cw.shape[0]
    ratio = BLOCK // LANES
    backward = lambda array: (
        array, pl.BlockSpec((array.shape[0], BLOCK), lambda b: (0, blocks - 1 - b))
    )
    tok = lambda rows, dtype: (
        out((rows, length), dtype), pl.BlockSpec((rows, BLOCK), lambda b: (0, blocks - 1 - b))
    )
    fixed = lambda shape: (
        out(shape, F32), pl.BlockSpec(shape, lambda b: (0,) * len(shape))
    )
    before = lambda b: (0, jnp.maximum(ratio * (blocks - 1 - b) - 1, 0))
    return call(
        states_back_kernel,
        (blocks,),
        [
            backward(u),
            (u, pl.BlockSpec((channels, LANES), before)),
            whole(halo),
            backward(step_low),
            backward(xs),
            backward(dy),
            backward(dx_local),
            backward(dbc_local),
            backward(bc),
            backward(dt),
            backward(w),
            backward(wt),
            backward(row_sums),
            (sin, pl.BlockSpec((1,) + sin.shape[1:], lambda b: (blocks - 1 - b, 0, 0))),
            whole(sdev),
            whole(dsend),
            whole(cw),
            whole(cb),
            whole(bias),
            whole(rate),
            whole(skip),
        ],
        [
            tok(channels, LOW),
            tok(heads, LOW),
            fixed((channels, LANES)),
            fixed((channels, LANES)),
            fixed((taps + 1, channels, LANES)),
            fixed((3, heads, BLOCK)),
        ],
        [
            pltpu.VMEM((inner, n_state), F32),
            pltpu.VMEM((inner, n_state), LOW),
            pltpu.VMEM((inner, n_state), LOW),
            pltpu.VMEM((inner, BLOCK), F32),
            pltpu.VMEM((inner, BLOCK), F32),
            pltpu.VMEM((inner, BLOCK), LOW),
            pltpu.VMEM((inner, BLOCK), LOW),
            pltpu.VMEM((heads, BLOCK), F32),
            pltpu.VMEM((heads, BLOCK), F32),
            pltpu.VMEM((heads, LANES), F32),
            pltpu.VMEM((heads, LANES), F32),
            pltpu.VMEM((heads, BLOCK), F32),
            pltpu.VMEM((heads, BLOCK), F32),
            pltpu.VMEM((heads, BLOCK), F32),
            pltpu.VMEM((heads, LANES), F32),
            pltpu.VMEM((channels, LANES), F32),
        ],
        2 * length * inner * n_state * 5,
        inner * length * 14 + taps * channels * 2048,
        3 * channels * length,
    )


def shifted(x, axis, by):
    devices = lax.axis_size(axis)
    return lax.ppermute(
        x, axis, [(i, i + by) for i in range(devices) if 0 <= i + by < devices]
    )


def swapped(x):
    return lax.ppermute(x, "section", [(0, 1), (1, 0)])


def chained(own, decays, toward):
    devices = lax.axis_size("head")
    index = lax.axis_index("head")
    everyone = lax.all_gather(own, "head", axis=0)
    factors = lax.all_gather(decays, "head", axis=0).astype(F32)
    inner = own.shape[0]
    heads = decays.shape[0]
    carried = jnp.zeros((heads, inner // heads, own.shape[1]), F32)
    order = range(devices) if toward == 1 else range(devices - 1, -1, -1)
    for m in order:
        before = (m < index) if toward == 1 else (m > index)
        term = everyone[m].astype(F32).reshape(carried.shape)
        moved = carried * factors[m][:, :1, None] + term
        carried = jnp.where(before, moved, carried)
    return carried.reshape(own.shape)


def gathered(shard):
    pair = lax.all_gather(shard, "section", axis=0)
    return [lax.all_gather(pair[i], ("seq", "head"), axis=0, tiled=True) for i in range(pair.shape[0])]


def summed_rows(parts):
    section = lax.axis_index("section")
    totals = []
    for part in parts:
        totals.append(lax.psum_scatter(part, ("seq", "head"), scatter_dimension=0, tiled=True))
    own = jnp.where(section == 0, totals[0], totals[1])
    other = jnp.where(section == 0, totals[1], totals[0])
    return own + swapped(other)


def rms_inverse(h):
    return lax.rsqrt(jnp.mean(h * h, axis=-1, keepdims=True) + EPSILON)


def spread(values, lanes):
    return jnp.broadcast_to(values[..., None], values.shape + (lanes,))


def layer_forward(h, p):
    inner, n_state = p["inner"], p["n_state"]
    channels = inner + 2 * n_state
    normed = (h * rms_inverse(h) * p["norm_gain"]).astype(LOW)
    w_in = p["w_in"]
    z = contract(w_in[:, :inner], normed, 0, 1)
    u = contract(w_in[:, inner : inner + channels], normed, 0, 1).astype(LOW)
    step_low = contract(w_in[:, inner + channels :], normed, 0, 1).astype(LOW)
    halo = shifted(u[:, -LANES:], "head", 1)
    xs, bc, dt, w, wt, wcol, sin, send = scan_states(
        u, halo, step_low, p["cw"], p["cb"], p["bias"], p["rate"], n_state
    )
    sdev = chained(send[:inner], send[inner:], 1).astype(LOW)
    y_local = scan_local(xs, bc, dt, w, wcol, sin)
    ylow, gated = gate_forward(y_local, xs, z, bc, wt, sdev, p["skip"], p["gate_gain"])
    result = h + contract(gated, p["w_out"], 0, 0)
    kept = dict(
        h=h, normed=normed, z=z, u=u, step_low=step_low, halo=halo, xs=xs, bc=bc, dt=dt, w=w, wt=wt,
        wcol=wcol, sin=sin, sdev=sdev, ylow=ylow, gated=gated, decays=send[inner:],
    )
    return result, kept


def layer_backward(g, p, k):
    inner, n_state = p["inner"], p["n_state"]
    channels = inner + 2 * n_state
    g_low = g.astype(LOW)
    dw_out = contract(k["gated"], g_low, 1, 0)
    dgated = contract(p["w_out"], g_low, 1, 1)
    dy, dz, gate_gain_grad, ds_own = gate_backward(
        dgated, k["ylow"], k["z"], k["bc"], k["wt"], p["gate_gain"]
    )
    dsend = chained(ds_own, k["decays"], -1)
    dx_local, row_sums, dbc_local = scan_local_back(
        k["xs"], dy, k["bc"], k["dt"], k["w"], k["wcol"]
    )
    du, dstep, first, last, gconv, ghead = scan_states_back(
        k["u"], k["halo"], k["step_low"], k["xs"], dy, dx_local, dbc_local, k["bc"], k["dt"], k["w"],
        k["wt"], row_sums, k["sin"], k["sdev"], dsend,
        p["cw"], p["cb"], p["bias"], p["rate"], p["skip"],
    )
    taps = p["cw"].shape[0]
    length = du.shape[1]
    ahead = shifted(first[:, : taps - 1], "head", -1)
    fix = last[:, LANES - (taps - 1) :]
    columns = []
    for back in range(taps - 1, 0, -1):
        value = fix[:, taps - 1 - back]
        for tap in range(taps - 1):
            place = taps - 1 - tap - back
            if place >= 0:
                value = value + p["cw"][tap, :, 0] * ahead[:, place]
        columns.append(value)
    du = lax.dynamic_update_slice(
        du, jnp.stack(columns, axis=1).astype(LOW), (0, length - (taps - 1))
    )
    w_in = p["w_in"]
    normed = k["normed"]
    dprojected = jnp.concatenate([dz, du, dstep], axis=0)
    dw_in = contract(normed, dprojected, 0, 1)
    dnormed = contract(dprojected, w_in, 0, 1)
    h = k["h"]
    r = rms_inverse(h)
    wd = dnormed * p["norm_gain"]
    dh = r * wd - h * (r * r * r * jnp.mean(wd * h, axis=-1, keepdims=True))
    norm_gain_grad = jnp.sum(dnormed * h * r, axis=0)
    small = dict(
        norm=norm_gain_grad,
        conv=jnp.sum(gconv, axis=2),
        head=jnp.sum(ghead, axis=2),
        gate=jnp.sum(gate_gain_grad, axis=1),
    )
    return g + dh, dw_in, dw_out, small


def local(
    section_ends, norm_gain, in_weight, conv_weight, conv_bias, dt_bias, a_log, skip_gain, gated_gain, out_weight,
):
    section = lax.axis_index("section")
    layers = lax.axis_size("section")
    inner = gated_gain.shape[1]
    heads = dt_bias.shape[1]
    n_state = (conv_bias.shape[1] - inner) // 2
    ends = section_ends[0, :, 0]
    received = swapped(jnp.where(section == 0, ends[1], ends[0]))
    hidden = jnp.where(section == 0, ends[0], received)
    cotangent = jnp.where(section == 0, received, ends[1])

    w_in = gathered(in_weight[0].astype(LOW))
    w_out = gathered(out_weight[0].astype(LOW))
    mine = (norm_gain, conv_weight, conv_bias, dt_bias, a_log, skip_gain, gated_gain)
    flat = jnp.concatenate([a.reshape(-1) for a in mine])
    both = lax.all_gather(flat, "section", axis=0)
    params = []
    for i in range(layers):
        parts, at = [], 0
        for a in mine:
            parts.append(both[i, at : at + a.size].reshape(a.shape[1:]))
            at += a.size
        gain, cw, cb, bias, alog, skip, gate_gain = parts
        params.append(
            dict(
                inner=inner,
                n_state=n_state,
                norm_gain=gain,
                w_in=w_in[i],
                w_out=w_out[i],
                cw=spread(cw, LANES),
                cb=spread(cb, LANES),
                bias=spread(bias, BLOCK),
                rate=spread(-jnp.exp(alog), BLOCK),
                skip=spread(skip, BLOCK),
                gate_gain=spread(gate_gain, LANES),
            )
        )

    kept = []
    for p in params:
        hidden, k = layer_forward(hidden, p)
        kept.append(k)
    grad = cotangent
    in_grads, out_grads, smalls = [None] * layers, [None] * layers, [None] * layers
    for i in range(layers - 1, -1, -1):
        grad, in_grads[i], out_grads[i], smalls[i] = layer_backward(grad, params[i], kept[i])

    other = swapped(jnp.where(section == 0, hidden, grad))
    ends_out = jnp.where(
        section == 0, jnp.stack([grad, other]), jnp.stack([other, hidden])
    )
    in_rows = summed_rows(in_grads)
    out_rows = summed_rows(out_grads)

    taps = conv_weight.shape[1]
    flat = jnp.stack(
        [
            jnp.concatenate(
                [s["norm"], s["conv"].reshape(-1), s["head"].reshape(-1), s["gate"]]
            )
            for s in smalls
        ]
    )
    total = lax.psum(flat, ("section", "seq", "head"))
    total = jnp.where(section == 0, total[0], total[1])
    shapes = [norm_gain, conv_weight, conv_bias, dt_bias, a_log, skip_gain, gated_gain]
    grads, at = [], 0
    for a in shapes:
        grads.append(total[at : at + a.size].reshape(a.shape))
        at += a.size
    norm_g, conv_g, shift_g, bias_g, alog_g, skip_g, gate_g = grads
    return (
        ends_out[None, :, None], norm_g, in_rows[None], conv_g, shift_g, bias_g, alog_g, skip_g, gate_g,
        out_rows[None],
    )


def solution(mesh):
    in_specs = (
        P("section", None, "seq", "head", None),
        P("section", None),
        P("section", ("seq", "head"), None),
        P("section", None, None),
        P("section", None),
        P("section", None),
        P("section", None),
        P("section", None),
        P("section", None),
        P("section", ("seq", "head"), None),
    )
    out_specs = in_specs
    return jax.shard_map(local, mesh=mesh, in_specs=in_specs, out_specs=out_specs, check_vma=False)
```

```python
import functools

import jax
import jax.numpy as jnp
from jax import lax
from jax.experimental import pallas as pl
from jax.experimental.pallas import tpu as pltpu
from jax.sharding import PartitionSpec as P

BLOCK = 128
GROUP = 4
SUBS = 2
EPSILON = 1e-05
LOG2E = 1.4426950408889634
HIGHEST = lax.Precision.HIGHEST
F32 = jnp.float32
LOW = jnp.bfloat16
VMEM_BYTES = 56 * 1024 * 1024


def contract(a, b, a_dim, b_dim, precision=None):
    return lax.dot_general(
        a, b, (((a_dim,), (b_dim,)), ((), ())), preferred_element_type=F32, precision=precision
    )


def sigmoid(v):
    return 0.5 * jnp.tanh(0.5 * v) + 0.5


def softplus(v):
    return jnp.maximum(v, 0.0) + jnp.log1p(jnp.exp(-jnp.abs(v)))


def ordered(transposed=False):
    row = lax.broadcasted_iota(jnp.int32, (BLOCK, BLOCK), 0)
    col = lax.broadcasted_iota(jnp.int32, (BLOCK, BLOCK), 1)
    return (row >= col) if transposed else (row <= col)


def fold(values):
    return jnp.sum(values.reshape(values.shape[0] // 8, 8, values.shape[1]), axis=0)


def column_sum(values):
    return jnp.sum(values, axis=0, keepdims=True)


def grouped(heads, width, body, unroll=8):
    size = GROUP if heads % GROUP == 0 else 1

    def step(g, carry):
        first = g * size
        rows = pl.ds(pl.multiple_of(first * width, size * width), size * width)
        parts = [(pl.ds(first + i, 1), slice(i * width, (i + 1) * width)) for i in range(size)]
        body(first, rows, parts)
        return carry

    lax.fori_loop(0, heads // size, step, 0, unroll=min(unroll, heads // size))


def spread_lanes(columns, place, target):
    target[...] = jnp.broadcast_to(columns[:, place : place + 1], target.shape)


def call(kernel, grid, ins, outs, scratch, flops, nbytes, transcendentals=0):
    arrays = [a for a, _ in ins]
    return pl.pallas_call(
        kernel,
        grid=grid,
        in_specs=[s for _, s in ins],
        out_specs=[s for _, s in outs],
        out_shape=[a for a, _ in outs],
        scratch_shapes=scratch,
        compiler_params=pltpu.CompilerParams(
            dimension_semantics=("arbitrary",) * len(grid), vmem_limit_bytes=VMEM_BYTES
        ),
        cost_estimate=pl.CostEstimate(
            flops=flops, bytes_accessed=nbytes, transcendentals=transcendentals
        ),
    )(*arrays)


def whole(array):
    rank = len(array.shape)
    return (
        array, pl.BlockSpec(array.shape, lambda b: (0,) * rank, pipeline_mode=pl.Buffered(1))
    )


def out(shape, dtype):
    return jax.ShapeDtypeStruct(shape, dtype)


def tokens(array, place=lambda b: b, rows=None, at=0):
    rows = array.shape[0] if rows is None else rows
    return (array, pl.BlockSpec((rows, BLOCK), lambda b: (at, place(b))))


def token_out(rows, length, dtype, place=lambda b: b):
    return (out((rows, length), dtype), pl.BlockSpec((rows, BLOCK), lambda b: (0, place(b))))


def fixed_out(shape, dtype):
    return (out(shape, dtype), pl.BlockSpec(shape, lambda b: (0,) * len(shape)))


def states_kernel(
    u_ref, halo_ref, step_ref, chan_ref, bias_ref, rate_ref,
    xs_ref, slope_ref, bc_ref, dt_ref, w_ref, wt_ref, wcol_ref, sin_ref, send_ref,
    tail, state, scale, ewend, offset, cw_ref, cb_ref,
):
    step = pl.program_id(0)
    heads = step_ref.shape[0]
    inner = xs_ref.shape[0]
    width = inner // heads
    taps = cw_ref.shape[0]
    n_state = bc_ref.shape[0] // 2

    @pl.when(step == 0)
    def _():
        for k in range(taps):
            spread_lanes(chan_ref, k, cw_ref.at[k])
        spread_lanes(chan_ref, taps, cb_ref)
        for k in range(taps - 1):
            tail[k] = pltpu.roll(halo_ref[...].astype(F32), taps - 1 - k, 1)
        state[...] = jnp.zeros_like(state)
        offset[...] = jnp.zeros_like(offset)

    dt = softplus(step_ref[...].astype(F32) + bias_ref[...])
    loga = dt * rate_ref[...]
    w = contract(loga, ordered().astype(F32), 1, 0, HIGHEST)
    wcol_ref[...] = contract(ordered(True).astype(F32), loga, 1, 1, HIGHEST)
    wend = jnp.broadcast_to(w[:, BLOCK - 1 :], w.shape)
    dt_ref[...] = dt
    w_ref[...] = w
    wt_ref[...] = w + offset[...]
    offset[...] += wend
    scale[...] = dt * jnp.exp(wend - w)
    ewend[...] = jnp.exp(wend)

    def conv(rows):
        u = u_ref[rows, :].astype(F32)
        lane = lax.broadcasted_iota(jnp.int32, (1, BLOCK), 1)
        c = cb_ref[rows, :] + cw_ref[taps - 1, rows, :] * u
        for k in range(taps - 1):
            back = taps - 1 - k
            rolled = pltpu.roll(u, back, 1)
            c = c + cw_ref[k, rows, :] * jnp.where(lane >= back, rolled, tail[k, rows, :])
            tail[k, rows, :] = rolled
        sig = sigmoid(c)
        value = c * sig
        slope_ref[rows, :] = (sig + value * (1.0 - sig)).astype(LOW)
        return value

    for i in range(2):
        bc_ref[i * n_state : (i + 1) * n_state, :] = conv(
            pl.ds(inner + i * n_state, n_state)
        ).astype(LOW)

    def group(first, rows, parts):
        xs = conv(rows)
        xs_ref[rows, :] = xs.astype(LOW)
        xd = jnp.concatenate([xs[own, :] * scale[h, :] for h, own in parts], axis=0).astype(LOW)
        fresh = contract(xd, bc_ref[:n_state, :], 1, 1)
        old = state[rows, :]
        sin_ref[0, rows, :] = old.astype(LOW)
        state[rows, :] = jnp.concatenate(
            [ewend[h, :] * old[own, :] + fresh[own, :] for h, own in parts], axis=0
        )

    grouped(heads, width, group)

    @pl.when(step == pl.num_programs(0) - 1)
    def _():
        send_ref[:inner, :] = state[...].astype(LOW)
        send_ref[inner:, :] = jnp.exp(offset[...]).astype(LOW)


def scan_states(u, chan, taps, bias, rate, heads, n_state):
    channels = chan.shape[0]
    length = u.shape[1] - BLOCK
    inner = channels - 2 * n_state
    blocks = length // BLOCK
    return call(
        states_kernel,
        (blocks,),
        [
            tokens(u, lambda b: b, channels),
            tokens(u, lambda b: blocks, channels),
            tokens(u, lambda b: b, heads, channels // heads),
            whole(chan), whole(bias), whole(rate),
        ],
        [
            token_out(inner, length, LOW),
            token_out(channels, length, LOW),
            token_out(2 * n_state, length, LOW),
            token_out(heads, length, F32),
            token_out(heads, length, F32),
            token_out(heads, length, F32),
            (out((length, heads), F32), pl.BlockSpec((BLOCK, heads), lambda b: (b, 0))),
            (
                out((blocks, inner, n_state), LOW),
                pl.BlockSpec((1, inner, n_state), lambda b: (b, 0, 0)),
            ),
            fixed_out((inner + heads, n_state), LOW),
        ],
        [
            pltpu.VMEM((taps - 1, channels, BLOCK), F32),
            pltpu.VMEM((inner, n_state), F32),
            pltpu.VMEM((heads, BLOCK), F32),
            pltpu.VMEM((heads, BLOCK), F32),
            pltpu.VMEM((heads, BLOCK), F32),
            pltpu.VMEM((taps, channels, BLOCK), F32),
            pltpu.VMEM((channels, BLOCK), F32),
        ],
        2 * length * inner * n_state,
        channels * length * 8,
        channels * length,
    )


def spread_columns(wcol_ref, wb):
    for h in range(wb.shape[0]):
        wb[h] = jnp.broadcast_to(wcol_ref[:, h : h + 1] * LOG2E, (BLOCK, BLOCK))


def masked_scores(bc_ref, n_state):
    scores = contract(bc_ref[:n_state, :], bc_ref[n_state:, :], 0, 0)
    return jnp.where(ordered(), scores, 0.0)


def decay(wrow, wb_h):
    return jnp.exp2(jnp.minimum(wrow * LOG2E - wb_h, 0.0))


def local_kernel(xs_ref, bc_ref, dt_ref, w_ref, wcol_ref, sin_ref, y_ref, wb, scores):
    heads = dt_ref.shape[0]
    inner = xs_ref.shape[0]
    width = inner // heads
    n_state = bc_ref.shape[0] // 2
    spread_columns(wcol_ref, wb)
    scores[...] = masked_scores(bc_ref, n_state)

    def group(first, rows, parts):
        entering = contract(sin_ref[0, rows, :], bc_ref[n_state:, :], 1, 0)
        xs = xs_ref[rows, :].astype(F32)
        result = []
        for i, (h, own) in enumerate(parts):
            wrow = w_ref[h, :]
            xdt = (xs[own, :] * dt_ref[h, :]).astype(LOW)
            weights = (scores[...] * decay(wrow, wb[first + i])).astype(LOW)
            result.append(entering[own, :] * jnp.exp(wrow) + contract(xdt, weights, 1, 0))
        y_ref[rows, :] = jnp.concatenate(result, axis=0).astype(y_ref.dtype)

    grouped(heads, width, group)


def scan_local(xs, bc, dt, w, wcol, sin):
    inner, length = xs.shape
    heads = dt.shape[0]
    return call(
        local_kernel,
        (length // BLOCK,),
        [
            tokens(xs),
            tokens(bc),
            tokens(dt),
            tokens(w),
            (wcol, pl.BlockSpec((BLOCK, heads), lambda b: (b, 0))),
            (sin, pl.BlockSpec((1,) + sin.shape[1:], lambda b: (b, 0, 0))),
        ],
        [token_out(inner, length, LOW)],
        [pltpu.VMEM((heads, BLOCK, BLOCK), F32), pltpu.VMEM((BLOCK, BLOCK), F32)],
        2 * length * inner * (BLOCK * 4 + bc.shape[0] // 2),
        inner * length * 6,
        heads * length * BLOCK,
    )[0]


def gate_kernel(
    yl_ref, xs_ref, z_ref, bc_ref, wt_ref, sdev_ref, skip_ref, gcol_ref,
    ylow_ref, halves_ref, gated_ref, v_scr, total, gain_ref, *, order,
):
    inner = yl_ref.shape[0]
    heads = wt_ref.shape[0]
    width = inner // heads
    half = width // 2
    n_state = bc_ref.shape[0] // 2
    total[...] = jnp.zeros_like(total)

    @pl.when(pl.program_id(0) == 0)
    def _():
        spread_lanes(gcol_ref, 0, gain_ref)

    def group(first, rows, parts):
        corr = contract(sdev_ref[rows, :], bc_ref[n_state:, :], 1, 0)
        xs = xs_ref[rows, :].astype(F32)
        extra = jnp.concatenate(
            [jnp.exp(wt_ref[h, :]) * corr[own, :] + skip_ref[h, :] * xs[own, :] for h, own in parts],
            axis=0,
        )
        y = (yl_ref[rows, :].astype(F32) + extra).astype(LOW)
        ylow_ref[rows, :] = y
        z = z_ref[rows, :].astype(F32)
        v = y.astype(F32) * (z * sigmoid(z))
        v_scr[rows, :] = v
        total[...] += fold(v * v)

    grouped(heads, width, group)
    r = lax.rsqrt(column_sum(total[...]) / inner + EPSILON)
    for h in range(heads):
        rows = slice(h * width, (h + 1) * width)
        gated = (v_scr[rows, :] * r * gain_ref[rows, :]).astype(LOW)
        for c in range(2):
            piece = gated[c * half : (c + 1) * half, :]
            halves_ref[c, h * half : (h + 1) * half, :] = piece
            if order is None:
                gated_ref[h * width + c * half : h * width + (c + 1) * half, :] = piece
            else:
                at = order[h][1] * half
                gated_ref[order[h][0], c, at : at + half, :] = piece


def gate_forward(yl, xs, z, bc, wt, sdev, skip, gain, order):
    inner, length = yl.shape
    heads = wt.shape[0]
    if order is None:
        gated = token_out(inner, length, LOW)
    else:
        shape = (2, 2, inner // 4)
        gated = (
            out(shape + (length,), LOW), pl.BlockSpec(shape + (BLOCK,), lambda b: (0, 0, 0, b))
        )
    pair = (2, inner // 2)
    halves = (out(pair + (length,), LOW), pl.BlockSpec(pair + (BLOCK,), lambda b: (0, 0, b)))
    return call(
        functools.partial(gate_kernel, order=order),
        (length // BLOCK,),
        [
            tokens(yl), tokens(xs), tokens(z), tokens(bc), tokens(wt), whole(sdev), whole(skip), whole(gain),
        ],
        [token_out(inner, length, LOW), halves, gated],
        [
            pltpu.VMEM((inner, BLOCK), F32),
            pltpu.VMEM((8, BLOCK), F32),
            pltpu.VMEM((inner, BLOCK), F32),
        ],
        2 * length * inner * sdev.shape[1],
        inner * length * 14,
        inner * length,
    )


def gate_back_kernel(
    dg0_ref, dg1_ref, ylow_ref, z_ref, bc_ref, wt_ref, gcol_ref, decays_ref,
    dy_ref, dz_ref, gsum_ref, send_ref, ds, gg, sums, sig_scr, dg_ref, gain_ref,
):
    step = pl.program_id(0)
    inner = ylow_ref.shape[0]
    heads = wt_ref.shape[0]
    width = inner // heads
    n_state = bc_ref.shape[0] // 2

    @pl.when(step == 0)
    def _():
        spread_lanes(gcol_ref, 0, gain_ref)
        gg[...] = jnp.zeros_like(gg)
        ds[...] = jnp.zeros_like(ds)

    sums[...] = jnp.zeros_like(sums)
    half = width // 2

    def first_pass(first, rows, parts):
        own = pl.ds(pl.multiple_of(first * half, len(parts) * half), len(parts) * half)
        both = [ref[own, :].astype(F32) for ref in (dg0_ref, dg1_ref)]
        dg_ref[rows, :] = jnp.concatenate(
            [both[c][i * half : (i + 1) * half, :] for i in range(len(parts)) for c in range(2)], axis=0
        )
        z = z_ref[rows, :].astype(F32)
        sig = sigmoid(z)
        sig_scr[rows, :] = sig
        v = ylow_ref[rows, :].astype(F32) * (z * sig)
        m = v * (dg_ref[rows, :] * gain_ref[rows, :])
        sums[0] += fold(v * v)
        sums[1] += fold(m)

    grouped(heads, width, first_pass)
    r = lax.rsqrt(column_sum(sums[0]) / inner + EPSILON)
    back = r * r * r * (column_sum(sums[1]) / inner)

    def second_pass(first, rows, parts):
        z = z_ref[rows, :].astype(F32)
        sig = sig_scr[rows, :]
        silu = z * sig
        y = ylow_ref[rows, :].astype(F32)
        v = y * silu
        du = dg_ref[rows, :]
        dv = r * (gain_ref[rows, :] * du) - v * back
        dy = (dv * silu).astype(LOW)
        dy_ref[rows, :] = dy
        dz_ref[rows, :] = (dv * y * (sig + silu * (1.0 - sig))).astype(LOW)
        gg[rows, :] += du * v * r
        dy = dy.astype(F32)
        dye = jnp.concatenate([dy[own, :] * jnp.exp(wt_ref[h, :]) for h, own in parts], axis=0)
        ds[rows, :] += contract(dye.astype(LOW), bc_ref[n_state:, :], 1, 1)

    grouped(heads, width, second_pass)

    @pl.when(step == pl.num_programs(0) - 1)
    def _():
        send_ref[:inner, :] = ds[...].astype(LOW)
        send_ref[inner:, :] = decays_ref[...]
        gsum_ref[:, 0:1] = jnp.sum(gg[...], axis=1, keepdims=True)


def gate_backward(dg0, dg1, ylow, z, bc, wt, gain, decays):
    inner, length = ylow.shape
    heads = wt.shape[0]
    n_state = bc.shape[0] // 2
    return call(
        gate_back_kernel,
        (length // BLOCK,),
        [
            tokens(dg0), tokens(dg1),
            tokens(ylow), tokens(z), tokens(bc), tokens(wt), whole(gain), whole(decays),
        ],
        [
            token_out(inner, length, LOW),
            token_out(inner, length, LOW),
            fixed_out((inner, 8), F32),
            fixed_out((inner + heads, n_state), LOW),
        ],
        [
            pltpu.VMEM((inner, n_state), F32),
            pltpu.VMEM((inner, BLOCK), F32),
            pltpu.VMEM((2, 8, BLOCK), F32),
            pltpu.VMEM((inner, BLOCK), F32),
            pltpu.VMEM((inner, BLOCK), F32),
            pltpu.VMEM((inner, BLOCK), F32),
        ],
        2 * length * inner * n_state,
        inner * length * 10,
        inner * length,
    )


def local_back_kernel(
    xs_ref, dy_ref, bc_ref, dt_ref, w_ref, wcol_ref, dx_ref, rows_ref, dbc_ref, wb, scores, dscores
):
    heads = dt_ref.shape[0]
    inner = xs_ref.shape[0]
    width = inner // heads
    n_state = bc_ref.shape[0] // 2
    spread_columns(wcol_ref, wb)
    scores[...] = masked_scores(bc_ref, n_state)
    dscores[...] = jnp.zeros_like(dscores)

    def group(first, rows, parts):
        xs = xs_ref[rows, :].astype(F32)
        dy_all = dy_ref[rows, :]
        result, total = [], 0.0
        for i, (h, own) in enumerate(parts):
            xdt = (xs[own, :] * dt_ref[h, :]).astype(LOW)
            dy = dy_all[own, :]
            decays = decay(w_ref[h, :], wb[first + i])
            weights = (scores[...] * decays).astype(LOW)
            y = contract(xdt, weights, 1, 0)
            dx = contract(dy, weights, 1, 1)
            total = total + decays * contract(xdt, dy, 0, 0)
            result.append(dx)
            rows_ref[h, :] = column_sum(dy.astype(F32) * y - xdt.astype(F32) * dx)
        dscores[...] += total
        dx_ref[rows, :] = jnp.concatenate(result, axis=0).astype(dx_ref.dtype)

    grouped(heads, width, group)
    masked = jnp.where(ordered(), dscores[...], 0.0).astype(LOW)
    dbc_ref[:n_state, :] = contract(bc_ref[n_state:, :], masked, 1, 1)
    dbc_ref[n_state:, :] = contract(bc_ref[:n_state, :], masked, 1, 0)


def scan_local_back(xs, dy, bc, dt, w, wcol):
    inner, length = xs.shape
    heads = dt.shape[0]
    return call(
        local_back_kernel,
        (length // BLOCK,),
        [
            tokens(xs),
            tokens(dy),
            tokens(bc),
            tokens(dt),
            tokens(w),
            (wcol, pl.BlockSpec((BLOCK, heads), lambda b: (b, 0))),
        ],
        [
            token_out(inner, length, LOW),
            token_out(heads, length, F32),
            token_out(bc.shape[0], length, F32),
        ],
        [
            pltpu.VMEM((heads, BLOCK, BLOCK), F32),
            pltpu.VMEM((BLOCK, BLOCK), F32),
            pltpu.VMEM((BLOCK, BLOCK), F32),
        ],
        2 * length * inner * BLOCK * 12,
        inner * length * 6,
        heads * length * BLOCK,
    )


def states_back_kernel(
    u_ref, halo_ref, step_ref, slope_ref, xs_ref, dy_ref, dxl_ref, dbcl_ref, bc_ref,
    dt_ref, w_ref, wt_ref, rows_ref, sin_ref, sdev_ref, dsend_ref,
    chan_ref, bias_ref, rate_ref, skip_ref,
    du_ref, first_ref, csum_ref, hsum_ref,
    ds, toend, ew, ewend, offs, rr, kk, ddt, ee, right, gconv, ghead, dbc, dc_first, cw_ref,
):
    step = pl.program_id(0)
    final = pl.num_programs(0) - 1
    heads = step_ref.shape[0]
    inner = xs_ref.shape[0]
    channels = u_ref.shape[0]
    width = inner // heads
    n_state = bc_ref.shape[0] // 2
    taps = cw_ref.shape[0]
    subs = sin_ref.shape[0]
    spans = [slice(s * BLOCK, (s + 1) * BLOCK) for s in range(subs)]
    backwards = list(reversed(range(subs)))

    @pl.when(step == 0)
    def _():
        ds[...] = dsend_ref[...]
        for k in range(taps):
            spread_lanes(chan_ref, k, cw_ref.at[k])
        right[...] = jnp.zeros_like(right)
        gconv[...] = jnp.zeros_like(gconv)
        ghead[...] = jnp.zeros_like(ghead)

    for s in range(subs):
        w = w_ref[:, spans[s]]
        wend = jnp.broadcast_to(w[:, BLOCK - 1 :], w.shape)
        toend[s] = jnp.exp(wend - w)
        ew[s] = jnp.exp(w)
        ewend[s] = jnp.exp(wend)
        offs[s] = jnp.exp(wt_ref[:, spans[s]] - w)
        dbc[s] = dbcl_ref[:, spans[s]]

    def conv_back(rows, dxs):
        lane = lax.broadcasted_iota(jnp.int32, (1, BLOCK), 1)
        carried = [right[k, rows, :] for k in range(taps - 1)]
        sums = [gconv[k, rows, :] for k in range(taps + 1)]
        for s in backwards:
            u = u_ref[rows, spans[s]].astype(F32)
            dc = dxs[s] * slope_ref[rows, spans[s]].astype(F32)
            du = cw_ref[taps - 1, rows, :] * dc
            sums[taps - 1] = sums[taps - 1] + u * dc
            sums[taps] = sums[taps] + dc
            for k in range(taps - 1):
                ahead = taps - 1 - k
                rolled = pltpu.roll(dc, BLOCK - ahead, 1)
                moved = jnp.where(lane < BLOCK - ahead, rolled, carried[k])
                carried[k] = rolled
                du = du + cw_ref[k, rows, :] * moved
                sums[k] = sums[k] + u * moved
            du_ref[rows, spans[s]] = du.astype(LOW)
        for k in range(taps - 1):
            right[k, rows, :] = carried[k]
        for k in range(taps + 1):
            gconv[k, rows, :] = sums[k]
        dc_first[rows, :] = dc

    def group(first, rows, parts):
        sdev = sdev_ref[rows, :].astype(F32)
        d = ds[rows, :]
        b_low = bc_ref[:n_state, :]
        c_low = bc_ref[n_state:, :]
        all_dxs = [None] * subs
        for s in backwards:
            sin = sin_ref[s, rows, :].astype(F32)
            entering = jnp.concatenate(
                [sin[own, :] + offs[s, h, :] * sdev[own, :] for h, own in parts], axis=0
            )
            cross = d * entering
            for h, own in parts:
                ee[s, h, :] = ewend[s, h, :] * column_sum(cross[own, :])
            d_low = d.astype(LOW)
            entering_low = entering.astype(LOW)
            q = contract(d_low, b_low[:, spans[s]], 1, 0)
            yo = contract(entering_low, c_low[:, spans[s]], 1, 0)
            xs = xs_ref[rows, spans[s]].astype(F32)
            dy = dy_ref[rows, spans[s]].astype(F32)
            dxl = dxl_ref[rows, spans[s]].astype(F32)
            xde, dye, dxs = [], [], []
            for h, own in parts:
                te, eh, dt = toend[s, h, :], ew[s, h, :], dt_ref[h, spans[s]]
                x, g = xs[own, :], dy[own, :]
                xe = x * dt * te
                ge = g * eh
                kk[s, h, :] = column_sum(xe * q[own, :])
                rr[s, h, :] = rows_ref[h, spans[s]] + column_sum(ge * yo[own, :])
                xde.append(xe)
                dye.append(ge)
                dx = dxl[own, :] + te * q[own, :]
                ddt[s, h, :] = column_sum(dx * x)
                ghead[2, h, :] += column_sum(g * x)
                dxs.append(dx * dt + skip_ref[h, :] * g)
            xde = jnp.concatenate(xde, axis=0).astype(LOW)
            dye = jnp.concatenate(dye, axis=0).astype(LOW)
            dbc[s, :n_state, :] += contract(d_low, xde, 0, 0)
            dbc[s, n_state:, :] += contract(entering_low, dye, 0, 0)
            fresh = contract(dye, c_low[:, spans[s]], 1, 1)
            d = jnp.concatenate(
                [ewend[s, h, :] * d[own, :] + fresh[own, :] for h, own in parts], axis=0
            )
            all_dxs[s] = jnp.concatenate(dxs, axis=0)
        ds[rows, :] = d
        conv_back(rows, all_dxs)

    grouped(heads, width, group)
    for i in range(2):
        at = slice(i * n_state, (i + 1) * n_state)
        conv_back(pl.ds(inner + i * n_state, n_state), [dbc[s, at, :] for s in range(subs)])

    upper = ordered().astype(F32)
    rate = rate_ref[...]
    for s in range(subs):
        dloga = (
            contract(rr[s], upper, 1, 1, HIGHEST)
            + (contract(kk[s], upper, 1, 0, HIGHEST) - kk[s])
            + jnp.sum(ee[s], axis=1, keepdims=True)
        )
        dt = dt_ref[:, spans[s]]
        raw = step_ref[:, spans[s]].astype(F32) + bias_ref[...]
        dstep = (ddt[s] + dloga * rate) * sigmoid(raw)
        du_ref[channels:, spans[s]] = dstep.astype(LOW)
        ghead[0] += dstep
        ghead[1] += dloga * dt * rate

    @pl.when(step == final)
    def _():
        first_ref[...] = dc_first[...].T[: first_ref.shape[0], :]
        lane = lax.broadcasted_iota(jnp.int32, (1, BLOCK), 1)
        size = channels // 8

        def sums(i, carry):
            rows = pl.ds(pl.multiple_of(i * size, 16), size)
            halo = halo_ref[rows, :].astype(F32)
            dc = dc_first[rows, :]
            for k in range(taps + 1):
                total = gconv[k, rows, :]
                if k < taps - 1:
                    back = taps - 1 - k
                    total = total + jnp.where(lane < back, pltpu.roll(halo, back, 1) * dc, 0.0)
                csum_ref[rows, k : k + 1] = jnp.sum(total, axis=1, keepdims=True)
            return carry

        lax.fori_loop(0, 8, sums, 0)
        for i in range(3):
            hsum_ref[:, i : i + 1] = jnp.sum(ghead[i], axis=1, keepdims=True)


def scan_states_back(
    u, slope, xs, dy, dx_local, dbc_local, bc, dt, w, wt, row_sums, sin, sdev, dsend,
    chan, taps, bias, rate, skip,
):
    channels, length = slope.shape
    heads = dt.shape[0]
    inner = xs.shape[0]
    steps = length // (SUBS * BLOCK)
    n_state = bc.shape[0] // 2
    span = SUBS * BLOCK
    place = lambda b: steps - 1 - b

    def pairs(array, rows=None, at=0):
        rows = array.shape[0] if rows is None else rows
        return (array, pl.BlockSpec((rows, span), lambda b: (at, place(b))))

    def pairs_out(rows, dtype):
        return (out((rows, length), dtype), pl.BlockSpec((rows, span), lambda b: (0, place(b))))

    per_head = pltpu.VMEM((SUBS, heads, BLOCK), F32)
    return call(
        states_back_kernel,
        (steps,),
        [
            pairs(u, channels),
            tokens(u, lambda b: length // BLOCK, channels),
            pairs(u, heads, channels // heads),
            pairs(slope),
            pairs(xs),
            pairs(dy),
            pairs(dx_local),
            pairs(dbc_local),
            pairs(bc),
            pairs(dt),
            pairs(w),
            pairs(wt),
            pairs(row_sums),
            (sin, pl.BlockSpec((SUBS,) + sin.shape[1:], lambda b: (place(b), 0, 0))),
            whole(sdev),
            whole(dsend),
            whole(chan),
            whole(bias),
            whole(rate),
            whole(skip),
        ],
        [
            pairs_out(channels + heads, LOW),
            fixed_out((8, channels), F32),
            fixed_out((channels, 8), F32),
            fixed_out((heads, 8), F32),
        ],
        [
            pltpu.VMEM((inner, n_state), F32),
            per_head,
            per_head,
            per_head,
            per_head,
            per_head,
            per_head,
            per_head,
            per_head,
            pltpu.VMEM((taps - 1, channels, BLOCK), F32),
            pltpu.VMEM((taps + 1, channels, BLOCK), F32),
            pltpu.VMEM((3, heads, BLOCK), F32),
            pltpu.VMEM((SUBS, 2 * n_state, BLOCK), F32),
            pltpu.VMEM((channels, BLOCK), F32),
            pltpu.VMEM((taps, channels, BLOCK), F32),
        ],
        2 * length * inner * n_state * 5,
        inner * length * 14 + taps * channels * 1024,
        channels * length,
    )


def edge_kernel(du_ref, ahead_ref, chan_ref, out_ref, *, taps):
    lanes = du_ref.shape[1]
    channels = ahead_ref.shape[1]
    lane = lax.broadcasted_iota(jnp.int32, (1, lanes), 1)
    for at in range(0, channels, lanes):
        rows = slice(at, at + lanes)
        ahead = jnp.concatenate(
            [ahead_ref[:, rows], jnp.zeros((lanes - ahead_ref.shape[0], lanes), F32)], axis=0
        ).T
        du = du_ref[rows, :].astype(F32)
        for k in range(taps - 1):
            back = taps - 1 - k
            moved = pltpu.roll(ahead, lanes - back, 1)
            du = du + jnp.where(lane >= lanes - back, chan_ref[rows, k : k + 1] * moved, 0.0)
        out_ref[rows, :] = du.astype(LOW)


def add_edge(du, ahead, chan, taps):
    channels = ahead.shape[1]
    last = du.shape[1] // BLOCK - 1
    block = pl.BlockSpec((channels, BLOCK), lambda b: (0, last))
    return pl.pallas_call(
        functools.partial(edge_kernel, taps=taps),
        grid=(1,),
        in_specs=[block, whole(ahead)[1], whole(chan)[1]],
        out_specs=block,
        out_shape=out(du.shape, LOW),
        input_output_aliases={0: 0},
        compiler_params=pltpu.CompilerParams(vmem_limit_bytes=VMEM_BYTES),
        cost_estimate=pl.CostEstimate(flops=0, bytes_accessed=channels * 3000, transcendentals=0),
    )(du, ahead, chan)


def shifted(x, axis, by):
    devices = lax.axis_size(axis)
    return lax.ppermute(
        x, axis, [(i, i + by) for i in range(devices) if 0 <= i + by < devices]
    )


def swapped(x):
    return lax.ppermute(x, "section", [(0, 1), (1, 0)])


def after(value, *others):
    return lax.optimization_barrier((value,) + others)[0]


def summed(value, axes):
    for axis in axes:
        reach = 1
        while reach < lax.axis_size(axis):
            pairs = [(i, i ^ reach) for i in range(lax.axis_size(axis))]
            value = value + lax.ppermute(value, axis, pairs)
            reach *= 2
    return value


def chained(own, inner, heads, toward):
    devices = lax.axis_size("head")
    shape = (heads, inner // heads, own.shape[1])
    split = lambda a: (a[:inner].astype(F32).reshape(shape), a[inner:].astype(F32)[:, :1, None])
    if devices <= 4:
        terms = [split(shifted(own, "head", toward * k)) for k in range(1, devices)]
        total = terms[-1][0]
        for state, factor in terms[-2::-1]:
            total = state + factor * total
        return total.reshape(inner, own.shape[1])
    index = lax.axis_index("head")
    everyone = lax.all_gather(own, "head", axis=0)
    total = jnp.zeros(shape, F32)
    for m in range(devices) if toward == 1 else range(devices - 1, -1, -1):
        state, factor = split(everyone[m])
        before = (m < index) if toward == 1 else (m > index)
        total = jnp.where(before, total * factor + state, total)
    return total.reshape(inner, own.shape[1])


def gathered(in_shard, out_shard, joined):
    section = lax.axis_index("section")
    layers = lax.axis_size("section")
    rows = in_shard.shape[0]
    model = out_shard.shape[1]
    across = ("seq", "head", "section")
    halves = lambda a: a.reshape((2, a.shape[0] // 2) + a.shape[1:])

    def pieces(a):
        a = halves(a)
        own = lax.dynamic_index_in_dim(a, section, 0, keepdims=False)
        got = swapped(lax.dynamic_index_in_dim(a, 1 - section, 0, keepdims=False))
        return [jnp.where(section == i, own, got) for i in range(layers)]

    everyone = lambda a: lax.all_gather(a, across, axis=0, tiled=True)
    result = []
    if joined:
        side = out_shard.reshape(2, 2, rows // 2, model).transpose(0, 2, 1, 3).reshape(rows, 2 * model)
        for piece in pieces(jnp.concatenate([side, in_shard], axis=1)):
            every = everyone(piece)
            result.append((every[:, : 2 * model], every[:, 2 * model :]))
        return result
    for in_piece, out_piece in zip(pieces(in_shard), pieces(out_shard)):
        w_in = everyone(in_piece)
        result.append((everyone(out_piece), w_in))
    return result


def products(left, rights, index):
    return jnp.concatenate(
        [
            contract(lax.dynamic_index_in_dim(a, index, 0, keepdims=False), b, 1, dim)
            for a, (b, dim) in zip(left, rights)
        ],
        axis=1,
    )


def pair_sent(left, rights):
    return products(left, rights, 1 - lax.axis_index("section")).astype(LOW)


def pair_sum(left, rights, sent):
    own = products(left, rights, lax.axis_index("section"))
    return (own + swapped(sent).astype(F32)).astype(LOW)


def over_head(part):
    count = lax.axis_size("head")
    rows, columns = part.shape
    part = lax.all_to_all(part, "head", split_axis=0, concat_axis=0, tiled=True)
    return jnp.sum(part.reshape(count, rows // count, columns).astype(F32), axis=0).astype(LOW)


def over_seq(part):
    count = lax.axis_size("seq")
    rows, columns = part.shape
    part = lax.all_to_all(part, "seq", split_axis=0, concat_axis=0, tiled=True)
    return jnp.sum(part.reshape(count, rows // count, columns).astype(F32), axis=0)


def over_both(part):
    return lax.psum_scatter(part, ("head", "seq"), scatter_dimension=0, tiled=True).astype(F32)


def by_owner(values, split):
    seqs, heads_n = lax.axis_size("seq"), lax.axis_size("head")
    rows, columns = values.shape
    own = rows // (seqs * heads_n * 2 * split)
    values = values.reshape(seqs, heads_n, 2, split, own, columns)
    return values.transpose(2, 3, 1, 0, 4, 5).reshape(2, split, seqs * heads_n * own, columns)


def rms_inverse(h):
    return lax.rsqrt(jnp.mean(h * h, axis=-1, keepdims=True) + EPSILON)


def spread(values):
    return jnp.broadcast_to(values[..., None], values.shape + (BLOCK,))


def columns(*vectors):
    rows = [v[None] for v in vectors]
    rows.append(jnp.zeros((8 - len(vectors), vectors[0].shape[0]), F32))
    return jnp.concatenate(rows, axis=0).T


def first_norm(h, p):
    normed = (h * rms_inverse(h) * p["norm_gain"]).astype(LOW)
    edge = shifted(after(h[-8:], *p["early"]), "head", 1)
    edge = (edge * rms_inverse(edge) * p["norm_gain"]).astype(LOW)
    padded = jnp.concatenate([normed, jnp.zeros((BLOCK - 8, h.shape[1]), LOW), edge], axis=0)
    return normed, padded


def layer_forward(h, normed, padded, p):
    inner, n_state, heads = p["inner"], p["n_state"], p["heads"]
    u = contract(p["w_x"], padded, 0, 1).astype(LOW)
    z = contract(p["w_z"], normed, 0, 1).astype(LOW)
    xs, slope, bc, dt, w, wt, wcol, sin, send = scan_states(
        u, p["chan"], p["taps"], p["bias"], p["rate"], heads, n_state
    )
    sdev = chained(send, inner, heads, 1).astype(LOW)
    y_local = scan_local(xs, bc, dt, w, wcol, sin)
    ylow, halves, gated = gate_forward(
        y_local, xs, z, bc, wt, sdev, p["skip"], p["gate_gain"], p["order"]
    )
    if p["order"] is None:
        gated = by_owner(gated, 2)
    result = h + contract(halves[0], p["w_o"][0], 0, 0) + contract(halves[1], p["w_o"][1], 0, 0)
    kept = dict(
        h=h, normed=normed, z=z, u=u, slope=slope, xs=xs, bc=bc, dt=dt, w=w, wt=wt,
        wcol=wcol, sin=sin, sdev=sdev, ylow=ylow, gated=gated, decays=send[inner:],
    )
    return result, kept


def layer_backward(g, p, k, finished, pending):
    inner, n_state, heads, last, taps = p["inner"], p["n_state"], p["heads"], p["last"], p["taps"]
    g_low = g.astype(LOW)
    dg = [contract(w, g_low, 1, 1).astype(LOW) for w in p["w_o"]]
    if last:
        pending = over_head(pending)
    normed_rows = by_owner(k["normed"].T, 1)[:, 0]
    dy, dz, gsum, send = gate_backward(
        dg[0], dg[1], k["ylow"], k["z"], k["bc"], k["wt"], p["gate_gain"], k["decays"]
    )
    left = [k["gated"][:, 0], k["gated"][:, 1], normed_rows]
    rights = [(g_low, 0), (g_low, 0), (after(dz, *finished), 1)]
    sent = pair_sent(left, rights)
    dsend = chained(send, inner, heads, -1)
    if last:
        sent = after(sent, pending)
        pending = over_seq(pending)
    dx_local, row_sums, dbc_local = scan_local_back(
        k["xs"], after(dy, sent), k["bc"], k["dt"], k["w"], k["wcol"]
    )
    early = pair_sum(left, rights, sent)
    du, first, csum, hsum = scan_states_back(
        k["u"], k["slope"], k["xs"], dy, after(dx_local, early), dbc_local, k["bc"], k["dt"], k["w"],
        k["wt"], row_sums, k["sin"], k["sdev"], dsend, p["chan"], p["taps"], p["bias"], p["rate"], p["skip"],
    )
    ahead = shifted(first, "head", -1)
    dnormed = contract(dz, p["w_z"], 0, 1)
    if last:
        early = over_head(after(early, dsend, dx_local, pending))
        du = after(du, early, dnormed)
        early = over_seq(early)
    else:
        early = over_both(early)
        du = after(du, dnormed)
    du = add_edge(du, ahead, p["chan"], taps)
    left, rights = [normed_rows], [(du, 1)]
    sent = pair_sent(left, rights)
    late = pair_sum(left, rights, after(sent, early) if last else sent)
    dnormed = dnormed + contract(after(du, late), p["w_x"], 0, 1)
    h = k["h"]
    r = rms_inverse(h)
    wd = dnormed * p["norm_gain"]
    dh = r * wd - h * (r * r * r * jnp.mean(wd * h, axis=-1, keepdims=True))
    small = jnp.concatenate(
        [
            jnp.sum(dnormed * h * r, axis=0),
            csum[:, : taps + 1].T.reshape(-1),
            hsum[:, :3].T.reshape(-1),
            gsum[:, 0],
        ]
    )
    return g + dh, early, late, pending, small


def local(
    section_ends, norm_gain, in_weight, conv_weight, conv_bias, dt_bias, a_log, skip_gain, gated_gain, out_weight,
):
    section = lax.axis_index("section")
    layers = lax.axis_size("section")
    seqs, heads_n = lax.axis_size("seq"), lax.axis_size("head")
    inner = gated_gain.shape[1]
    heads = dt_bias.shape[1]
    width = inner // heads
    n_state = (conv_bias.shape[1] - inner) // 2
    model = norm_gain.shape[1]
    ends = section_ends[0, :, 0]
    turned = jnp.where(section == 0, ends[1], ends[0])
    received = swapped(turned)
    hidden = jnp.where(section == 0, ends[0], received)
    cotangent = jnp.where(section == 0, received, ends[1])

    joined = out_weight.shape[1] == 2 * width and in_weight.shape[1] == width
    weights = gathered(in_weight[0].astype(LOW), out_weight[0].astype(LOW), joined)
    mine = (norm_gain, conv_weight, conv_bias, dt_bias, a_log, skip_gain, gated_gain)
    flat = jnp.concatenate([a.reshape(-1) for a in mine])
    other = swapped(flat)
    params = []
    for i in range(layers):
        own = jnp.where(section == i, flat, other)
        parts, at = [], 0
        for a in mine:
            parts.append(own[at : at + a.size].reshape(a.shape[1:]))
            at += a.size
        gain, cw, cb, bias, alog, skip, gate_gain = parts
        w_out, w_in = weights[i]
        order = tuple((h % 2, (h // 2 % heads_n) * seqs + h // 2 // heads_n) for h in range(heads))
        if joined:
            w_o = (w_out[:, :model], w_out[:, model:])
        else:
            w_o = w_out.reshape(heads, 2, width // 2, model).transpose(1, 0, 2, 3)
            w_o = w_o.reshape(2, inner // 2, model)
        params.append(
            dict(
                inner=inner,
                n_state=n_state,
                heads=heads,
                order=order if joined else None,
                last=i == 0,
                norm_gain=gain,
                w_z=w_in[:, :inner],
                w_x=w_in[:, inner:],
                w_o=w_o,
                taps=cw.shape[0],
                chan=columns(*cw, cb),
                bias=spread(bias),
                rate=spread(-jnp.exp(alog)),
                skip=spread(skip),
                gate_gain=columns(gate_gain),
            )
        )

    prepared = [p[name] for p in params for name in ("chan", "bias", "rate", "skip", "gate_gain")]
    params[0]["early"] = prepared
    params[1]["early"] = []
    kept = []
    for p in params:
        hidden, k = layer_forward(hidden, *first_norm(hidden, p), p)
        kept.append(k)
    hidden_other = lax.ppermute(hidden, "section", [(0, 1)])
    grad = after(cotangent, hidden)
    grad, early_1, late_1, _, small_1 = layer_backward(grad, params[1], kept[1], [], None)
    grad, early_0, late_0, late_1, small_0 = layer_backward(
        grad, params[0], kept[0], [early_1], late_1
    )
    grad_other = lax.ppermute(grad, "section", [(1, 0)])
    first = section == 0
    ends_out = jnp.stack(
        [jnp.where(first, grad, hidden_other), jnp.where(first, grad_other, hidden)]
    )

    total = jnp.where(first, small_0, small_1) + swapped(jnp.where(first, small_1, small_0))
    total = summed(total, ("head", "seq"))
    late_0 = over_seq(over_head(late_0))
    rows = [
        jnp.concatenate([early_0, after(late_0, total)], axis=1),
        jnp.concatenate([early_1, late_1], axis=1),
    ]
    got = swapped(jnp.where(first, rows[1], rows[0]))
    own = jnp.where(first, rows[0], rows[1])
    both = jnp.stack([jnp.where(first, own, got), jnp.where(first, got, own)])
    share = both.shape[1]
    out_rows = both[:, :, : 2 * model].reshape(2, share, 2, model).transpose(0, 2, 1, 3)
    out_rows = out_rows.reshape(4 * share, model)
    in_rows = both[:, :, 2 * model :].reshape(2 * share, -1)

    grads, at = [], 0
    for a in (norm_gain, conv_weight, conv_bias, dt_bias, a_log, skip_gain, gated_gain):
        grads.append(total[at : at + a.size].reshape(a.shape))
        at += a.size
    norm_g, conv_g, shift_g, bias_g, alog_g, skip_g, gate_g = grads
    return (
        ends_out[None, :, None], norm_g, in_rows[None], conv_g, shift_g, bias_g, alog_g, skip_g, gate_g,
        out_rows[None],
    )


def solution(mesh):
    in_specs = (
        P("section", None, "seq", "head", None),
        P("section", None),
        P("section", ("seq", "head"), None),
        P("section", None, None),
        P("section", None),
        P("section", None),
        P("section", None),
        P("section", None),
        P("section", None),
        P("section", ("seq", "head"), None),
    )
    return jax.shard_map(local, mesh=mesh, in_specs=in_specs, out_specs=in_specs, check_vma=False)
```

```python
import functools

import jax
import jax.numpy as jnp
from jax import lax
from jax.experimental import pallas as pl
from jax.experimental.pallas import tpu as pltpu
from jax.sharding import PartitionSpec as P

BLOCK = 128
GROUP = 4
SUBS = 2
EPSILON = 1e-05
LOG2E = 1.4426950408889634
HIGHEST = lax.Precision.HIGHEST
F32 = jnp.float32
LOW = jnp.bfloat16
VMEM_BYTES = 56 * 1024 * 1024


def contract(a, b, a_dim, b_dim, precision=None):
    return lax.dot_general(
        a, b, (((a_dim,), (b_dim,)), ((), ())), preferred_element_type=F32, precision=precision
    )


def sigmoid(v):
    return 0.5 * jnp.tanh(0.5 * v) + 0.5


def softplus(v):
    return jnp.maximum(v, 0.0) + jnp.log1p(jnp.exp(-jnp.abs(v)))


def ordered(transposed=False):
    row = lax.broadcasted_iota(jnp.int32, (BLOCK, BLOCK), 0)
    col = lax.broadcasted_iota(jnp.int32, (BLOCK, BLOCK), 1)
    return (row >= col) if transposed else (row <= col)


def fold(values):
    return jnp.sum(values.reshape(values.shape[0] // 8, 8, values.shape[1]), axis=0)


def column_sum(values):
    return jnp.sum(values, axis=0, keepdims=True)


def grouped(heads, width, body, unroll=8):
    size = GROUP if heads % GROUP == 0 else 1

    def step(g, carry):
        first = g * size
        rows = pl.ds(pl.multiple_of(first * width, size * width), size * width)
        parts = [(pl.ds(first + i, 1), slice(i * width, (i + 1) * width)) for i in range(size)]
        body(first, rows, parts)
        return carry

    lax.fori_loop(0, heads // size, step, 0, unroll=min(unroll, heads // size))


def spread_lanes(columns, place, target):
    target[...] = jnp.broadcast_to(columns[:, place : place + 1], target.shape)


def call(kernel, grid, ins, outs, scratch, flops, nbytes, transcendentals=0):
    arrays = [a for a, _ in ins]
    return pl.pallas_call(
        kernel,
        grid=grid,
        in_specs=[s for _, s in ins],
        out_specs=[s for _, s in outs],
        out_shape=[a for a, _ in outs],
        scratch_shapes=scratch,
        compiler_params=pltpu.CompilerParams(
            dimension_semantics=("arbitrary",) * len(grid), vmem_limit_bytes=VMEM_BYTES
        ),
        cost_estimate=pl.CostEstimate(
            flops=flops, bytes_accessed=nbytes, transcendentals=transcendentals
        ),
    )(*arrays)


def whole(array):
    rank = len(array.shape)
    return (
        array, pl.BlockSpec(array.shape, lambda b: (0,) * rank, pipeline_mode=pl.Buffered(1))
    )


def out(shape, dtype):
    return jax.ShapeDtypeStruct(shape, dtype)


def tokens(array, place=lambda b: b, rows=None, at=0):
    rows = array.shape[0] if rows is None else rows
    return (array, pl.BlockSpec((rows, BLOCK), lambda b: (at, place(b))))


def token_out(rows, length, dtype, place=lambda b: b):
    return (out((rows, length), dtype), pl.BlockSpec((rows, BLOCK), lambda b: (0, place(b))))


def fixed_out(shape, dtype):
    return (out(shape, dtype), pl.BlockSpec(shape, lambda b: (0,) * len(shape)))


def states_kernel(
    u_ref, halo_ref, step_ref, chan_ref, bias_ref, rate_ref,
    xs_ref, slope_ref, bc_ref, dt_ref, w_ref, wt_ref, wcol_ref, sin_ref, send_ref,
    tail, state, scale, ewend, offset, cw_ref, cb_ref,
):
    step = pl.program_id(0)
    heads = step_ref.shape[0]
    inner = xs_ref.shape[0]
    width = inner // heads
    taps = cw_ref.shape[0]
    n_state = bc_ref.shape[0] // 2

    @pl.when(step == 0)
    def _():
        for k in range(taps):
            spread_lanes(chan_ref, k, cw_ref.at[k])
        spread_lanes(chan_ref, taps, cb_ref)
        for k in range(taps - 1):
            tail[k] = pltpu.roll(halo_ref[...].astype(F32), taps - 1 - k, 1)
        state[...] = jnp.zeros_like(state)
        offset[...] = jnp.zeros_like(offset)

    dt = softplus(step_ref[...].astype(F32) + bias_ref[...])
    loga = dt * rate_ref[...]
    w = contract(loga, ordered().astype(F32), 1, 0, HIGHEST)
    wcol_ref[...] = contract(ordered(True).astype(F32), loga, 1, 1, HIGHEST)
    wend = jnp.broadcast_to(w[:, BLOCK - 1 :], w.shape)
    dt_ref[...] = dt
    w_ref[...] = w
    wt_ref[...] = w + offset[...]
    offset[...] += wend
    scale[...] = dt * jnp.exp(wend - w)
    ewend[...] = jnp.exp(wend)

    def conv(rows):
        u = u_ref[rows, :].astype(F32)
        lane = lax.broadcasted_iota(jnp.int32, (1, BLOCK), 1)
        c = cb_ref[rows, :] + cw_ref[taps - 1, rows, :] * u
        for k in range(taps - 1):
            back = taps - 1 - k
            rolled = pltpu.roll(u, back, 1)
            c = c + cw_ref[k, rows, :] * jnp.where(lane >= back, rolled, tail[k, rows, :])
            tail[k, rows, :] = rolled
        sig = sigmoid(c)
        value = c * sig
        slope_ref[rows, :] = (sig + value * (1.0 - sig)).astype(LOW)
        return value

    for i in range(2):
        bc_ref[i * n_state : (i + 1) * n_state, :] = conv(
            pl.ds(inner + i * n_state, n_state)
        ).astype(LOW)

    def group(first, rows, parts):
        xs = conv(rows)
        xs_ref[rows, :] = xs.astype(LOW)
        xd = jnp.concatenate([xs[own, :] * scale[h, :] for h, own in parts], axis=0).astype(LOW)
        fresh = contract(xd, bc_ref[:n_state, :], 1, 1)
        old = state[rows, :]
        sin_ref[0, rows, :] = old.astype(LOW)
        state[rows, :] = jnp.concatenate(
            [ewend[h, :] * old[own, :] + fresh[own, :] for h, own in parts], axis=0
        )

    grouped(heads, width, group)

    @pl.when(step == pl.num_programs(0) - 1)
    def _():
        send_ref[:inner, :] = state[...].astype(LOW)
        send_ref[inner:, :] = jnp.exp(offset[...]).astype(LOW)


def scan_states(u, chan, taps, bias, rate, heads, n_state):
    channels = chan.shape[0]
    length = u.shape[1] - BLOCK
    inner = channels - 2 * n_state
    blocks = length // BLOCK
    return call(
        states_kernel,
        (blocks,),
        [
            tokens(u, lambda b: b, channels),
            tokens(u, lambda b: blocks, channels),
            tokens(u, lambda b: b, heads, channels // heads),
            whole(chan), whole(bias), whole(rate),
        ],
        [
            token_out(inner, length, LOW),
            token_out(channels, length, LOW),
            token_out(2 * n_state, length, LOW),
            token_out(heads, length, F32),
            token_out(heads, length, F32),
            token_out(heads, length, F32),
            (out((length, heads), F32), pl.BlockSpec((BLOCK, heads), lambda b: (b, 0))),
            (
                out((blocks, inner, n_state), LOW),
                pl.BlockSpec((1, inner, n_state), lambda b: (b, 0, 0)),
            ),
            fixed_out((inner + heads, n_state), LOW),
        ],
        [
            pltpu.VMEM((taps - 1, channels, BLOCK), F32),
            pltpu.VMEM((inner, n_state), F32),
            pltpu.VMEM((heads, BLOCK), F32),
            pltpu.VMEM((heads, BLOCK), F32),
            pltpu.VMEM((heads, BLOCK), F32),
            pltpu.VMEM((taps, channels, BLOCK), F32),
            pltpu.VMEM((channels, BLOCK), F32),
        ],
        2 * length * inner * n_state,
        channels * length * 8,
        channels * length,
    )


def spread_columns(wcol_ref, wb):
    for h in range(wb.shape[0]):
        wb[h] = jnp.broadcast_to(wcol_ref[:, h : h + 1] * LOG2E, (BLOCK, BLOCK))


def masked_scores(bc_ref, n_state):
    scores = contract(bc_ref[:n_state, :], bc_ref[n_state:, :], 0, 0)
    return jnp.where(ordered(), scores, 0.0)


def decay(wrow, wb_h):
    return jnp.exp2(jnp.minimum(wrow * LOG2E - wb_h, 0.0))


def local_kernel(xs_ref, bc_ref, dt_ref, w_ref, wcol_ref, sin_ref, y_ref, wb, scores):
    heads = dt_ref.shape[0]
    inner = xs_ref.shape[0]
    width = inner // heads
    n_state = bc_ref.shape[0] // 2
    spread_columns(wcol_ref, wb)
    scores[...] = masked_scores(bc_ref, n_state)

    def group(first, rows, parts):
        entering = contract(sin_ref[0, rows, :], bc_ref[n_state:, :], 1, 0)
        xs = xs_ref[rows, :].astype(F32)
        result = []
        for i, (h, own) in enumerate(parts):
            wrow = w_ref[h, :]
            xdt = (xs[own, :] * dt_ref[h, :]).astype(LOW)
            weights = (scores[...] * decay(wrow, wb[first + i])).astype(LOW)
            result.append(entering[own, :] * jnp.exp(wrow) + contract(xdt, weights, 1, 0))
        y_ref[rows, :] = jnp.concatenate(result, axis=0).astype(y_ref.dtype)

    grouped(heads, width, group)


def scan_local(xs, bc, dt, w, wcol, sin):
    inner, length = xs.shape
    heads = dt.shape[0]
    return call(
        local_kernel,
        (length // BLOCK,),
        [
            tokens(xs),
            tokens(bc),
            tokens(dt),
            tokens(w),
            (wcol, pl.BlockSpec((BLOCK, heads), lambda b: (b, 0))),
            (sin, pl.BlockSpec((1,) + sin.shape[1:], lambda b: (b, 0, 0))),
        ],
        [token_out(inner, length, LOW)],
        [pltpu.VMEM((heads, BLOCK, BLOCK), F32), pltpu.VMEM((BLOCK, BLOCK), F32)],
        2 * length * inner * (BLOCK * 4 + bc.shape[0] // 2),
        inner * length * 6,
        heads * length * BLOCK,
    )[0]


def gate_kernel(
    yl_ref, xs_ref, z_ref, bc_ref, wt_ref, sdev_ref, skip_ref, gain_ref,
    ylow_ref, halves_ref, gated_ref, v_scr, total, *, order,
):
    inner = yl_ref.shape[0]
    heads = wt_ref.shape[0]
    width = inner // heads
    half = width // 2
    n_state = bc_ref.shape[0] // 2
    total[...] = jnp.zeros_like(total)

    def group(first, rows, parts):
        corr = contract(sdev_ref[rows, :], bc_ref[n_state:, :], 1, 0)
        xs = xs_ref[rows, :].astype(F32)
        extra = jnp.concatenate(
            [jnp.exp(wt_ref[h, :]) * corr[own, :] + skip_ref[h, :] * xs[own, :] for h, own in parts],
            axis=0,
        )
        y = (yl_ref[rows, :].astype(F32) + extra).astype(LOW)
        ylow_ref[rows, :] = y
        z = z_ref[rows, :].astype(F32)
        v = y.astype(F32) * (z * sigmoid(z))
        v_scr[rows, :] = v
        total[...] += fold(v * v)

    grouped(heads, width, group)
    r = lax.rsqrt(column_sum(total[...]) / inner + EPSILON)
    for h in range(heads):
        rows = slice(h * width, (h + 1) * width)
        gated = (v_scr[rows, :] * r * gain_ref[rows, :]).astype(LOW)
        for c in range(2):
            piece = gated[c * half : (c + 1) * half, :]
            halves_ref[c, h * half : (h + 1) * half, :] = piece
            if order is None:
                gated_ref[h * width + c * half : h * width + (c + 1) * half, :] = piece
            else:
                at = order[h][1] * half
                gated_ref[order[h][0], c, at : at + half, :] = piece


def gate_forward(yl, xs, z, bc, wt, sdev, skip, gain, order):
    inner, length = yl.shape
    heads = wt.shape[0]
    if order is None:
        gated = token_out(inner, length, LOW)
    else:
        shape = (2, 2, inner // 4)
        gated = (
            out(shape + (length,), LOW), pl.BlockSpec(shape + (BLOCK,), lambda b: (0, 0, 0, b))
        )
    pair = (2, inner // 2)
    halves = (out(pair + (length,), LOW), pl.BlockSpec(pair + (BLOCK,), lambda b: (0, 0, b)))
    return call(
        functools.partial(gate_kernel, order=order),
        (length // BLOCK,),
        [
            tokens(yl), tokens(xs), tokens(z), tokens(bc), tokens(wt), whole(sdev), whole(skip), whole(gain),
        ],
        [token_out(inner, length, LOW), halves, gated],
        [
            pltpu.VMEM((inner, BLOCK), F32),
            pltpu.VMEM((8, BLOCK), F32),
        ],
        2 * length * inner * sdev.shape[1],
        inner * length * 14,
        inner * length,
    )


def gate_back_kernel(
    dg0_ref, dg1_ref, ylow_ref, z_ref, bc_ref, wt_ref, gain_ref, decays_ref,
    dy_ref, dz_ref, gsum_ref, send_ref, ds, gg, sums, sig_scr, dg_ref,
):
    step = pl.program_id(0)
    inner = ylow_ref.shape[0]
    heads = wt_ref.shape[0]
    width = inner // heads
    n_state = bc_ref.shape[0] // 2

    @pl.when(step == 0)
    def _():
        gg[...] = jnp.zeros_like(gg)
        ds[...] = jnp.zeros_like(ds)

    sums[...] = jnp.zeros_like(sums)
    half = width // 2

    def first_pass(first, rows, parts):
        own = pl.ds(pl.multiple_of(first * half, len(parts) * half), len(parts) * half)
        both = [ref[own, :].astype(F32) for ref in (dg0_ref, dg1_ref)]
        dg_ref[rows, :] = jnp.concatenate(
            [both[c][i * half : (i + 1) * half, :] for i in range(len(parts)) for c in range(2)], axis=0
        )
        z = z_ref[rows, :].astype(F32)
        sig = sigmoid(z)
        sig_scr[rows, :] = sig
        v = ylow_ref[rows, :].astype(F32) * (z * sig)
        m = v * (dg_ref[rows, :] * gain_ref[rows, :])
        sums[0] += fold(v * v)
        sums[1] += fold(m)

    grouped(heads, width, first_pass)
    r = lax.rsqrt(column_sum(sums[0]) / inner + EPSILON)
    back = r * r * r * (column_sum(sums[1]) / inner)

    def second_pass(first, rows, parts):
        z = z_ref[rows, :].astype(F32)
        sig = sig_scr[rows, :]
        silu = z * sig
        y = ylow_ref[rows, :].astype(F32)
        v = y * silu
        du = dg_ref[rows, :]
        dv = r * (gain_ref[rows, :] * du) - v * back
        dy = (dv * silu).astype(LOW)
        dy_ref[rows, :] = dy
        dz_ref[rows, :] = (dv * y * (sig + silu * (1.0 - sig))).astype(LOW)
        gg[rows, :] += du * v * r
        dy = dy.astype(F32)
        dye = jnp.concatenate([dy[own, :] * jnp.exp(wt_ref[h, :]) for h, own in parts], axis=0)
        ds[rows, :] += contract(dye.astype(LOW), bc_ref[n_state:, :], 1, 1)

    grouped(heads, width, second_pass)

    @pl.when(step == pl.num_programs(0) - 1)
    def _():
        send_ref[:inner, :] = ds[...].astype(LOW)
        send_ref[inner:, :] = decays_ref[...]
        gsum_ref[:, 0:1] = jnp.sum(gg[...], axis=1, keepdims=True)


def gate_backward(dg0, dg1, ylow, z, bc, wt, gain, decays):
    inner, length = ylow.shape
    heads = wt.shape[0]
    n_state = bc.shape[0] // 2
    return call(
        gate_back_kernel,
        (length // BLOCK,),
        [
            tokens(dg0), tokens(dg1),
            tokens(ylow), tokens(z), tokens(bc), tokens(wt), whole(gain), whole(decays),
        ],
        [
            token_out(inner, length, LOW),
            token_out(inner, length, LOW),
            fixed_out((inner, 8), F32),
            fixed_out((inner + heads, n_state), LOW),
        ],
        [
            pltpu.VMEM((inner, n_state), F32),
            pltpu.VMEM((inner, BLOCK), F32),
            pltpu.VMEM((2, 8, BLOCK), F32),
            pltpu.VMEM((inner, BLOCK), F32),
            pltpu.VMEM((inner, BLOCK), F32),
        ],
        0,
        0,
    )


def local_back_kernel(
    xs_ref, dy_ref, bc_ref, dt_ref, w_ref, wcol_ref, dx_ref, rows_ref, dbc_ref, wb, scores, dscores
):
    heads = dt_ref.shape[0]
    inner = xs_ref.shape[0]
    width = inner // heads
    n_state = bc_ref.shape[0] // 2
    spread_columns(wcol_ref, wb)
    scores[...] = masked_scores(bc_ref, n_state)
    dscores[...] = jnp.zeros_like(dscores)

    def group(first, rows, parts):
        xs = xs_ref[rows, :].astype(F32)
        dy_all = dy_ref[rows, :]
        result, total = [], 0.0
        for i, (h, own) in enumerate(parts):
            xdt = (xs[own, :] * dt_ref[h, :]).astype(LOW)
            dy = dy_all[own, :]
            decays = decay(w_ref[h, :], wb[first + i])
            weights = (scores[...] * decays).astype(LOW)
            y = contract(xdt, weights, 1, 0)
            dx = contract(dy, weights, 1, 1)
            total = total + decays * contract(xdt, dy, 0, 0)
            result.append(dx)
            rows_ref[h, :] = column_sum(dy.astype(F32) * y - xdt.astype(F32) * dx)
        dscores[...] += total
        dx_ref[rows, :] = jnp.concatenate(result, axis=0).astype(dx_ref.dtype)

    grouped(heads, width, group)
    masked = jnp.where(ordered(), dscores[...], 0.0).astype(LOW)
    dbc_ref[:n_state, :] = contract(bc_ref[n_state:, :], masked, 1, 1)
    dbc_ref[n_state:, :] = contract(bc_ref[:n_state, :], masked, 1, 0)


def scan_local_back(xs, dy, bc, dt, w, wcol):
    inner, length = xs.shape
    heads = dt.shape[0]
    return call(
        local_back_kernel,
        (length // BLOCK,),
        [
            tokens(xs),
            tokens(dy),
            tokens(bc),
            tokens(dt),
            tokens(w),
            (wcol, pl.BlockSpec((BLOCK, heads), lambda b: (b, 0))),
        ],
        [
            token_out(inner, length, LOW),
            token_out(heads, length, F32),
            token_out(bc.shape[0], length, F32),
        ],
        [
            pltpu.VMEM((heads, BLOCK, BLOCK), F32),
            pltpu.VMEM((BLOCK, BLOCK), F32),
            pltpu.VMEM((BLOCK, BLOCK), F32),
        ],
        2 * length * inner * BLOCK * 12,
        inner * length * 6,
        heads * length * BLOCK,
    )


def states_back_kernel(
    u_ref, halo_ref, step_ref, slope_ref, xs_ref, dy_ref, dxl_ref, dbcl_ref, bc_ref,
    dt_ref, w_ref, wt_ref, rows_ref, sin_ref, sdev_ref, dsend_ref,
    chan_ref, bias_ref, rate_ref, skip_ref,
    du_ref, first_ref, csum_ref, hsum_ref,
    ds, toend, ew, ewend, offs, rr, kk, ddt, ee, right, gconv, ghead, dbc, dc_first, cw_ref,
):
    step = pl.program_id(0)
    final = pl.num_programs(0) - 1
    heads = step_ref.shape[0]
    inner = xs_ref.shape[0]
    channels = u_ref.shape[0]
    width = inner // heads
    n_state = bc_ref.shape[0] // 2
    taps = cw_ref.shape[0]
    subs = sin_ref.shape[0]
    spans = [slice(s * BLOCK, (s + 1) * BLOCK) for s in range(subs)]
    backwards = list(reversed(range(subs)))

    @pl.when(step == 0)
    def _():
        ds[...] = dsend_ref[...]
        for k in range(taps):
            spread_lanes(chan_ref, k, cw_ref.at[k])
        right[...] = jnp.zeros_like(right)
        gconv[...] = jnp.zeros_like(gconv)
        ghead[...] = jnp.zeros_like(ghead)

    for s in range(subs):
        w = w_ref[:, spans[s]]
        wend = jnp.broadcast_to(w[:, BLOCK - 1 :], w.shape)
        toend[s] = jnp.exp(wend - w)
        ew[s] = jnp.exp(w)
        ewend[s] = jnp.exp(wend)
        offs[s] = jnp.exp(wt_ref[:, spans[s]] - w)
        dbc[s] = dbcl_ref[:, spans[s]]

    def conv_back(rows, dxs):
        lane = lax.broadcasted_iota(jnp.int32, (1, BLOCK), 1)
        carried = [right[k, rows, :] for k in range(taps - 1)]
        sums = [gconv[k, rows, :] for k in range(taps + 1)]
        for s in backwards:
            u = u_ref[rows, spans[s]].astype(F32)
            dc = dxs[s] * slope_ref[rows, spans[s]].astype(F32)
            du = cw_ref[taps - 1, rows, :] * dc
            sums[taps - 1] = sums[taps - 1] + u * dc
            sums[taps] = sums[taps] + dc
            for k in range(taps - 1):
                ahead = taps - 1 - k
                rolled = pltpu.roll(dc, BLOCK - ahead, 1)
                moved = jnp.where(lane < BLOCK - ahead, rolled, carried[k])
                carried[k] = rolled
                du = du + cw_ref[k, rows, :] * moved
                sums[k] = sums[k] + u * moved
            du_ref[rows, spans[s]] = du.astype(LOW)
        for k in range(taps - 1):
            right[k, rows, :] = carried[k]
        for k in range(taps + 1):
            gconv[k, rows, :] = sums[k]
        dc_first[rows, :] = dc

    def group(first, rows, parts):
        sdev = sdev_ref[rows, :].astype(F32)
        d = ds[rows, :]
        b_low = bc_ref[:n_state, :]
        c_low = bc_ref[n_state:, :]
        all_dxs = [None] * subs
        for s in backwards:
            sin = sin_ref[s, rows, :].astype(F32)
            entering = jnp.concatenate(
                [sin[own, :] + offs[s, h, :] * sdev[own, :] for h, own in parts], axis=0
            )
            cross = d * entering
            for h, own in parts:
                ee[s, h, :] = ewend[s, h, :] * column_sum(cross[own, :])
            d_low = d.astype(LOW)
            entering_low = entering.astype(LOW)
            q = contract(d_low, b_low[:, spans[s]], 1, 0)
            yo = contract(entering_low, c_low[:, spans[s]], 1, 0)
            xs = xs_ref[rows, spans[s]].astype(F32)
            dy = dy_ref[rows, spans[s]].astype(F32)
            dxl = dxl_ref[rows, spans[s]].astype(F32)
            xde, dye, dxs = [], [], []
            for h, own in parts:
                te, eh, dt = toend[s, h, :], ew[s, h, :], dt_ref[h, spans[s]]
                x, g = xs[own, :], dy[own, :]
                xe = x * dt * te
                ge = g * eh
                kk[s, h, :] = column_sum(xe * q[own, :])
                rr[s, h, :] = rows_ref[h, spans[s]] + column_sum(ge * yo[own, :])
                xde.append(xe)
                dye.append(ge)
                dx = dxl[own, :] + te * q[own, :]
                ddt[s, h, :] = column_sum(dx * x)
                ghead[2, h, :] += column_sum(g * x)
                dxs.append(dx * dt + skip_ref[h, :] * g)
            xde = jnp.concatenate(xde, axis=0).astype(LOW)
            dye = jnp.concatenate(dye, axis=0).astype(LOW)
            dbc[s, :n_state, :] += contract(d_low, xde, 0, 0)
            dbc[s, n_state:, :] += contract(entering_low, dye, 0, 0)
            fresh = contract(dye, c_low[:, spans[s]], 1, 1)
            d = jnp.concatenate(
                [ewend[s, h, :] * d[own, :] + fresh[own, :] for h, own in parts], axis=0
            )
            all_dxs[s] = jnp.concatenate(dxs, axis=0)
        ds[rows, :] = d
        conv_back(rows, all_dxs)

    grouped(heads, width, group)
    for i in range(2):
        at = slice(i * n_state, (i + 1) * n_state)
        conv_back(pl.ds(inner + i * n_state, n_state), [dbc[s, at, :] for s in range(subs)])

    upper = ordered().astype(F32)
    rate = rate_ref[...]
    for s in range(subs):
        dloga = (
            contract(rr[s], upper, 1, 1, HIGHEST)
            + (contract(kk[s], upper, 1, 0, HIGHEST) - kk[s])
            + jnp.sum(ee[s], axis=1, keepdims=True)
        )
        dt = dt_ref[:, spans[s]]
        raw = step_ref[:, spans[s]].astype(F32) + bias_ref[...]
        dstep = (ddt[s] + dloga * rate) * sigmoid(raw)
        du_ref[channels:, spans[s]] = dstep.astype(LOW)
        ghead[0] += dstep
        ghead[1] += dloga * dt * rate

    @pl.when(step == final)
    def _():
        first_ref[...] = dc_first[...].T[: first_ref.shape[0], :]
        lane = lax.broadcasted_iota(jnp.int32, (1, BLOCK), 1)
        size = channels // 8

        def sums(i, carry):
            rows = pl.ds(pl.multiple_of(i * size, 16), size)
            halo = halo_ref[rows, :].astype(F32)
            dc = dc_first[rows, :]
            for k in range(taps + 1):
                total = gconv[k, rows, :]
                if k < taps - 1:
                    back = taps - 1 - k
                    total = total + jnp.where(lane < back, pltpu.roll(halo, back, 1) * dc, 0.0)
                csum_ref[rows, k : k + 1] = jnp.sum(total, axis=1, keepdims=True)
            return carry

        lax.fori_loop(0, 8, sums, 0)
        for i in range(3):
            hsum_ref[:, i : i + 1] = jnp.sum(ghead[i], axis=1, keepdims=True)


def scan_states_back(
    u, slope, xs, dy, dx_local, dbc_local, bc, dt, w, wt, row_sums, sin, sdev, dsend,
    chan, taps, bias, rate, skip,
):
    channels, length = slope.shape
    heads = dt.shape[0]
    inner = xs.shape[0]
    steps = length // (SUBS * BLOCK)
    n_state = bc.shape[0] // 2
    span = SUBS * BLOCK
    place = lambda b: steps - 1 - b

    def pairs(array, rows=None, at=0):
        rows = array.shape[0] if rows is None else rows
        return (array, pl.BlockSpec((rows, span), lambda b: (at, place(b))))

    def pairs_out(rows, dtype):
        return (out((rows, length), dtype), pl.BlockSpec((rows, span), lambda b: (0, place(b))))

    per_head = pltpu.VMEM((SUBS, heads, BLOCK), F32)
    return call(
        states_back_kernel,
        (steps,),
        [
            pairs(u, channels),
            tokens(u, lambda b: length // BLOCK, channels),
            pairs(u, heads, channels // heads),
            pairs(slope),
            pairs(xs),
            pairs(dy),
            pairs(dx_local),
            pairs(dbc_local),
            pairs(bc),
            pairs(dt),
            pairs(w),
            pairs(wt),
            pairs(row_sums),
            (sin, pl.BlockSpec((SUBS,) + sin.shape[1:], lambda b: (place(b), 0, 0))),
            whole(sdev),
            whole(dsend),
            whole(chan),
            whole(bias),
            whole(rate),
            whole(skip),
        ],
        [
            pairs_out(channels + heads, LOW),
            fixed_out((8, channels), F32),
            fixed_out((channels, 8), F32),
            fixed_out((heads, 8), F32),
        ],
        [
            pltpu.VMEM((inner, n_state), F32),
            per_head,
            per_head,
            per_head,
            per_head,
            per_head,
            per_head,
            per_head,
            per_head,
            pltpu.VMEM((taps - 1, channels, BLOCK), F32),
            pltpu.VMEM((taps + 1, channels, BLOCK), F32),
            pltpu.VMEM((3, heads, BLOCK), F32),
            pltpu.VMEM((SUBS, 2 * n_state, BLOCK), F32),
            pltpu.VMEM((channels, BLOCK), F32),
            pltpu.VMEM((taps, channels, BLOCK), F32),
        ],
        2 * length * inner * n_state * 5,
        inner * length * 14 + taps * channels * 1024,
        channels * length,
    )


def edge_kernel(du_ref, ahead_ref, chan_ref, out_ref, *, taps):
    lanes = du_ref.shape[1]
    channels = ahead_ref.shape[1]
    lane = lax.broadcasted_iota(jnp.int32, (1, lanes), 1)
    for at in range(0, channels, lanes):
        rows = slice(at, at + lanes)
        ahead = jnp.concatenate(
            [ahead_ref[:, rows], jnp.zeros((lanes - ahead_ref.shape[0], lanes), F32)], axis=0
        ).T
        du = du_ref[rows, :].astype(F32)
        for k in range(taps - 1):
            back = taps - 1 - k
            moved = pltpu.roll(ahead, lanes - back, 1)
            du = du + jnp.where(lane >= lanes - back, chan_ref[rows, k : k + 1] * moved, 0.0)
        out_ref[rows, :] = du.astype(LOW)


def add_edge(du, ahead, chan, taps):
    channels = ahead.shape[1]
    last = du.shape[1] // BLOCK - 1
    block = pl.BlockSpec((channels, BLOCK), lambda b: (0, last))
    return pl.pallas_call(
        functools.partial(edge_kernel, taps=taps),
        grid=(1,),
        in_specs=[block, whole(ahead)[1], whole(chan)[1]],
        out_specs=block,
        out_shape=out(du.shape, LOW),
        input_output_aliases={0: 0},
        compiler_params=pltpu.CompilerParams(vmem_limit_bytes=VMEM_BYTES),
        cost_estimate=pl.CostEstimate(flops=0, bytes_accessed=channels * 3000, transcendentals=0),
    )(du, ahead, chan)


def shifted(x, axis, by):
    devices = lax.axis_size(axis)
    return lax.ppermute(
        x, axis, [(i, i + by) for i in range(devices) if 0 <= i + by < devices]
    )


def swapped(x):
    return lax.ppermute(x, "section", [(0, 1), (1, 0)])


def after(value, *others):
    return lax.optimization_barrier((value,) + others)[0]


def summed(value, axes):
    for axis in axes:
        reach = 1
        while reach < lax.axis_size(axis):
            pairs = [(i, i ^ reach) for i in range(lax.axis_size(axis))]
            value = value + lax.ppermute(value, axis, pairs)
            reach *= 2
    return value


def chained(own, inner, heads, toward, beside):
    devices = lax.axis_size("head")
    shape = (heads, inner // heads, own.shape[1])
    split = lambda a: (a[:inner].astype(F32).reshape(shape), a[inner:].astype(F32)[:, :1, None])
    if devices <= 4:
        got = [shifted(own, "head", toward * k) for k in range(1, devices)]
        terms = [split(a) for a in lax.optimization_barrier((*got, beside))[:-1]]
        total = terms[-1][0]
        for state, factor in terms[-2::-1]:
            total = state + factor * total
        return total.reshape(inner, own.shape[1])
    index = lax.axis_index("head")
    everyone = lax.all_gather(own, "head", axis=0)
    total = jnp.zeros(shape, F32)
    for m in range(devices) if toward == 1 else range(devices - 1, -1, -1):
        state, factor = split(everyone[m])
        before = (m < index) if toward == 1 else (m > index)
        total = jnp.where(before, total * factor + state, total)
    return total.reshape(inner, own.shape[1])


def gathered(in_shard, out_shard, joined):
    section = lax.axis_index("section")
    layers = lax.axis_size("section")
    rows = in_shard.shape[0]
    model = out_shard.shape[1]
    across = ("seq", "head", "section")
    halves = lambda a: a.reshape((2, a.shape[0] // 2) + a.shape[1:])

    def pieces(a):
        a = halves(a)
        own = lax.dynamic_index_in_dim(a, section, 0, keepdims=False)
        got = swapped(lax.dynamic_index_in_dim(a, 1 - section, 0, keepdims=False))
        return [jnp.where(section == i, own, got) for i in range(layers)]

    everyone = lambda a: lax.all_gather(a, across, axis=0, tiled=True)
    result = []
    if joined:
        side = out_shard.reshape(2, 2, rows // 2, model).transpose(0, 2, 1, 3).reshape(rows, 2 * model)
        first, *others = pieces(jnp.concatenate([side, in_shard], axis=1))
        every = everyone(first)
        result.append((lambda since: every[:, : 2 * model], every[:, 2 * model :]))
        for piece in others:
            w_in = everyone(piece[:, 2 * model :])
            result.append(
                (lambda since, piece=piece: everyone(after(piece[:, : 2 * model], since)), w_in)
            )
        return result
    for in_piece, out_piece in zip(pieces(in_shard), pieces(out_shard)):
        w_in = everyone(in_piece)
        result.append((lambda since, out_piece=out_piece: everyone(out_piece), w_in))
    return result


def products(left, rights, index):
    return jnp.concatenate(
        [
            contract(lax.dynamic_index_in_dim(a, index, 0, keepdims=False), b, 1, dim)
            for a, (b, dim) in zip(left, rights)
        ],
        axis=1,
    )


def pair_sent(left, rights):
    return products(left, rights, 1 - lax.axis_index("section")).astype(LOW)


def pair_sum(left, rights, sent):
    own = products(left, rights, lax.axis_index("section"))
    return (own + swapped(sent).astype(F32)).astype(LOW)


def over_head(part, beside=()):
    count = lax.axis_size("head")
    rows, columns = part.shape
    part = after(lax.all_to_all(part, "head", split_axis=0, concat_axis=0, tiled=True), *beside)
    return jnp.sum(part.reshape(count, rows // count, columns).astype(F32), axis=0).astype(LOW)


def over_seq(part, beside=()):
    count = lax.axis_size("seq")
    rows, columns = part.shape
    part = after(lax.all_to_all(part, "seq", split_axis=0, concat_axis=0, tiled=True), *beside)
    return jnp.sum(part.reshape(count, rows // count, columns).astype(F32), axis=0)


def over_both(part):
    return lax.psum_scatter(part, ("head", "seq"), scatter_dimension=0, tiled=True).astype(F32)


def by_owner(values, split):
    seqs, heads_n = lax.axis_size("seq"), lax.axis_size("head")
    rows, columns = values.shape
    own = rows // (seqs * heads_n * 2 * split)
    values = values.reshape(seqs, heads_n, 2, split, own, columns)
    return values.transpose(2, 3, 1, 0, 4, 5).reshape(2, split, seqs * heads_n * own, columns)


def rms_inverse(h):
    return lax.rsqrt(jnp.mean(h * h, axis=-1, keepdims=True) + EPSILON)


def spread(values):
    return jnp.broadcast_to(values[..., None], values.shape + (BLOCK,))


def columns(*vectors):
    rows = [v[None] for v in vectors]
    rows.append(jnp.zeros((8 - len(vectors), vectors[0].shape[0]), F32))
    return jnp.concatenate(rows, axis=0).T


def first_norm(h, p):
    normed = (h * rms_inverse(h) * p["norm_gain"]).astype(LOW)
    edge = shifted(after(h[-8:], *p["early"]), "head", 1)
    edge = (edge * rms_inverse(edge) * p["norm_gain"]).astype(LOW)
    padded = jnp.concatenate([normed, jnp.zeros((BLOCK - 8, h.shape[1]), LOW), edge], axis=0)
    return normed, padded


def layer_forward(h, normed, padded, p):
    inner, n_state, heads = p["inner"], p["n_state"], p["heads"]
    u = contract(p["w_x"], padded, 0, 1).astype(LOW)
    z = contract(p["w_z"], normed, 0, 1).astype(LOW)
    xs, slope, bc, dt, w, wt, wcol, sin, send = scan_states(
        u, p["chan"], p["taps"], p["bias"], p["rate"], heads, n_state
    )
    y_local = scan_local(xs, bc, dt, w, wcol, sin)
    sdev = chained(send, inner, heads, 1, y_local).astype(LOW)
    ylow, halves, gated = gate_forward(
        y_local, xs, z, bc, wt, sdev, p["skip"], p["gate_gain"], p["order"]
    )
    if p["order"] is None:
        gated = by_owner(gated, 2)
    result = h + contract(halves[0], p["w_o"][0], 0, 0) + contract(halves[1], p["w_o"][1], 0, 0)
    kept = dict(
        h=h, normed_rows=by_owner(normed.T, 1)[:, 0], z=z, u=u, slope=slope, xs=xs, bc=bc, dt=dt, w=w, wt=wt,
        wcol=wcol, sin=sin, sdev=sdev, ylow=ylow, gated=gated, decays=send[inner:],
    )
    return result, kept


def layer_backward(g, p, k, finished, pending):
    inner, n_state, heads, last, taps = p["inner"], p["n_state"], p["heads"], p["last"], p["taps"]
    g_low = after(g.astype(LOW), *finished)
    dg = [contract(w, g_low, 1, 1).astype(LOW) for w in p["w_o"]]
    if last:
        pending = over_head(pending)
    normed_rows = k["normed_rows"]
    dy, dz, gsum, send = gate_backward(
        dg[0], dg[1], k["ylow"], k["z"], k["bc"], k["wt"], p["gate_gain"], k["decays"]
    )
    left = [k["gated"][:, 0], k["gated"][:, 1], normed_rows]
    rights = [(g_low, 0), (g_low, 0), (dz, 1)]
    sent = pair_sent(left, rights)
    if last:
        sent = after(sent, pending)
    dx_local, row_sums, dbc_local = scan_local_back(
        k["xs"], after(dy, sent), k["bc"], k["dt"], k["w"], k["wcol"]
    )
    if last:
        pending = over_seq(pending, (dx_local,))
    dsend = chained(send, inner, heads, -1, dx_local)
    early = pair_sum(left, rights, sent)
    du, first, csum, hsum = scan_states_back(
        k["u"], k["slope"], k["xs"], dy, after(dx_local, early), dbc_local, k["bc"], k["dt"], k["w"],
        k["wt"], row_sums, k["sin"], k["sdev"], dsend, p["chan"], p["taps"], p["bias"], p["rate"], p["skip"],
    )
    ahead = shifted(first, "head", -1)
    dnormed = contract(after(dz, first), p["w_z"], 0, 1)
    if last:
        early = over_head(after(early, dsend, dx_local, pending), (dnormed,))
        du = after(du, early, dnormed)
        early = over_seq(early)
    else:
        early = over_both(early)
        du = after(du, dnormed)
    du = add_edge(du, ahead, p["chan"], taps)
    left, rights = [normed_rows], [(du, 1)]
    sent = pair_sent(left, rights)
    late = pair_sum(left, rights, after(sent, early) if last else sent)
    dnormed = dnormed + contract(after(du, late), p["w_x"], 0, 1)
    h = k["h"]
    r = rms_inverse(h)
    wd = dnormed * p["norm_gain"]
    dh = r * wd - h * (r * r * r * jnp.mean(wd * h, axis=-1, keepdims=True))
    small = jnp.concatenate(
        [
            jnp.sum(dnormed * h * r, axis=0),
            csum[:, : taps + 1].T.reshape(-1),
            hsum[:, :3].T.reshape(-1),
            gsum[:, 0],
        ]
    )
    return g + dh, early, late, pending, small


def local(
    section_ends, norm_gain, in_weight, conv_weight, conv_bias, dt_bias, a_log, skip_gain, gated_gain, out_weight,
):
    section = lax.axis_index("section")
    layers = lax.axis_size("section")
    seqs, heads_n = lax.axis_size("seq"), lax.axis_size("head")
    inner = gated_gain.shape[1]
    heads = dt_bias.shape[1]
    width = inner // heads
    n_state = (conv_bias.shape[1] - inner) // 2
    model = norm_gain.shape[1]
    ends = section_ends[0, :, 0]
    turned = jnp.where(section == 0, ends[1], ends[0])
    received = swapped(turned)
    hidden = jnp.where(section == 0, ends[0], received)
    cotangent = jnp.where(section == 0, received, ends[1])

    joined = out_weight.shape[1] == 2 * width and in_weight.shape[1] == width
    weights = gathered(in_weight[0].astype(LOW), out_weight[0].astype(LOW), joined)
    mine = (norm_gain, conv_weight, conv_bias, dt_bias, a_log, skip_gain, gated_gain)
    flat = jnp.concatenate([a.reshape(-1) for a in mine])
    other = swapped(flat)
    params = []
    for i in range(layers):
        own = jnp.where(section == i, flat, other)
        parts, at = [], 0
        for a in mine:
            parts.append(own[at : at + a.size].reshape(a.shape[1:]))
            at += a.size
        gain, cw, cb, bias, alog, skip, gate_gain = parts
        w_out, w_in = weights[i]
        order = tuple((h % 2, (h // 2 % heads_n) * seqs + h // 2 // heads_n) for h in range(heads))
        params.append(
            dict(
                inner=inner,
                n_state=n_state,
                heads=heads,
                order=order if joined else None,
                last=i == 0,
                norm_gain=gain,
                w_z=w_in[:, :inner],
                w_x=w_in[:, inner:],
                w_out=w_out,
                taps=cw.shape[0],
                chan=columns(*cw, cb),
                bias=spread(bias),
                rate=spread(-jnp.exp(alog)),
                skip=spread(skip),
                gate_gain=spread(gate_gain),
            )
        )

    prepared = [p[name] for p in params for name in ("chan", "bias", "rate", "skip", "gate_gain")]
    params[0]["early"] = prepared
    params[1]["early"] = []
    kept = []
    for p in params:
        normed, padded = first_norm(hidden, p)
        if kept:
            padded = after(padded, kept[-1]["normed_rows"])
        w_out = p["w_out"](kept[-1]["u"] if kept else None)
        if joined:
            p["w_o"] = (w_out[:, :model], w_out[:, model:])
        else:
            w_o = w_out.reshape(heads, 2, width // 2, model).transpose(1, 0, 2, 3)
            p["w_o"] = w_o.reshape(2, inner // 2, model)
        hidden, k = layer_forward(hidden, normed, padded, p)
        kept.append(k)
    hidden_other = lax.ppermute(hidden, "section", [(0, 1)])
    grad = after(cotangent, hidden)
    grad, early_1, late_1, _, small_1 = layer_backward(grad, params[1], kept[1], [], None)
    grad, early_0, late_0, late_1, small_0 = layer_backward(
        grad, params[0], kept[0], [early_1], late_1
    )
    grad_other = lax.ppermute(grad, "section", [(1, 0)])
    first = section == 0
    ends_out = jnp.stack(
        [jnp.where(first, grad, hidden_other), jnp.where(first, grad_other, hidden)]
    )

    total = jnp.where(first, small_0, small_1) + swapped(jnp.where(first, small_1, small_0))
    total = summed(total, ("head", "seq"))
    grads, at = [], 0
    for a in (norm_gain, conv_weight, conv_bias, dt_bias, a_log, skip_gain, gated_gain):
        grads.append(total[at : at + a.size].reshape(a.shape))
        at += a.size
    norm_g, conv_g, shift_g, bias_g, alog_g, skip_g, gate_g = grads
    late_0 = over_seq(over_head(late_0))
    rows = [
        jnp.concatenate([early_0, after(late_0, *grads)], axis=1),
        jnp.concatenate([early_1, late_1], axis=1),
    ]
    got = swapped(jnp.where(first, rows[1], rows[0]))
    own = jnp.where(first, rows[0], rows[1])
    both = jnp.stack([jnp.where(first, own, got), jnp.where(first, got, own)])
    share = both.shape[1]
    out_rows = both[:, :, : 2 * model].reshape(2, share, 2, model).transpose(0, 2, 1, 3)
    out_rows = out_rows.reshape(4 * share, model)
    in_rows = both[:, :, 2 * model :].reshape(2 * share, -1)

    return (
        ends_out[None, :, None], norm_g, in_rows[None], conv_g, shift_g, bias_g, alog_g, skip_g, gate_g,
        out_rows[None],
    )


def solution(mesh):
    in_specs = (
        P("section", None, "seq", "head", None),
        P("section", None),
        P("section", ("seq", "head"), None),
        P("section", None, None),
        P("section", None),
        P("section", None),
        P("section", None),
        P("section", None),
        P("section", None),
        P("section", ("seq", "head"), None),
    )
    return jax.shard_map(local, mesh=mesh, in_specs=in_specs, out_specs=in_specs, check_vma=False)
```

```python
import functools

import jax
import jax.numpy as jnp
from jax import lax
from jax.experimental import pallas as pl
from jax.experimental.pallas import tpu as pltpu
from jax.sharding import PartitionSpec as P

BLOCK = 128
GROUP = 4
SUBS = 2
EPSILON = 1e-05
LOG2E = 1.4426950408889634
HIGHEST = lax.Precision.HIGHEST
F32 = jnp.float32
LOW = jnp.bfloat16
VMEM_BYTES = 56 * 1024 * 1024


def contract(a, b, a_dim, b_dim, precision=None):
    return lax.dot_general(
        a, b, (((a_dim,), (b_dim,)), ((), ())), preferred_element_type=F32, precision=precision
    )


def sigmoid(v):
    return 0.5 * jnp.tanh(0.5 * v) + 0.5


def softplus(v):
    return jnp.maximum(v, 0.0) + jnp.log1p(jnp.exp(-jnp.abs(v)))


def ordered(transposed=False):
    row = lax.broadcasted_iota(jnp.int32, (BLOCK, BLOCK), 0)
    col = lax.broadcasted_iota(jnp.int32, (BLOCK, BLOCK), 1)
    return (row >= col) if transposed else (row <= col)


def fold(values):
    return jnp.sum(values.reshape(values.shape[0] // 8, 8, values.shape[1]), axis=0)


def column_sum(values):
    return jnp.sum(values, axis=0, keepdims=True)


def grouped(heads, width, body, unroll=8):
    size = GROUP if heads % GROUP == 0 else 1

    def step(g, carry):
        first = g * size
        rows = pl.ds(pl.multiple_of(first * width, size * width), size * width)
        parts = [(pl.ds(first + i, 1), slice(i * width, (i + 1) * width)) for i in range(size)]
        body(first, rows, parts)
        return carry

    lax.fori_loop(0, heads // size, step, 0, unroll=min(unroll, heads // size))


def spread_lanes(columns, place, target):
    target[...] = jnp.broadcast_to(columns[:, place : place + 1], target.shape)


def call(kernel, grid, ins, outs, scratch, flops, nbytes, transcendentals=0):
    arrays = [a for a, _ in ins]
    return pl.pallas_call(
        kernel,
        grid=grid,
        in_specs=[s for _, s in ins],
        out_specs=[s for _, s in outs],
        out_shape=[a for a, _ in outs],
        scratch_shapes=scratch,
        compiler_params=pltpu.CompilerParams(
            dimension_semantics=("arbitrary",) * len(grid), vmem_limit_bytes=VMEM_BYTES
        ),
        cost_estimate=pl.CostEstimate(
            flops=flops, bytes_accessed=nbytes, transcendentals=transcendentals
        ),
    )(*arrays)


def whole(array):
    rank = len(array.shape)
    return (
        array, pl.BlockSpec(array.shape, lambda b: (0,) * rank, pipeline_mode=pl.Buffered(1))
    )


def out(shape, dtype):
    return jax.ShapeDtypeStruct(shape, dtype)


def tokens(array, place=lambda b: b, rows=None, at=0):
    rows = array.shape[0] if rows is None else rows
    return (array, pl.BlockSpec((rows, BLOCK), lambda b: (at, place(b))))


def token_out(rows, length, dtype, place=lambda b: b):
    return (out((rows, length), dtype), pl.BlockSpec((rows, BLOCK), lambda b: (0, place(b))))


def fixed_out(shape, dtype):
    return (out(shape, dtype), pl.BlockSpec(shape, lambda b: (0,) * len(shape)))


def states_kernel(
    u_ref, halo_ref, step_ref, chan_ref, bias_ref, rate_ref,
    xs_ref, slope_ref, bc_ref, dt_ref, w_ref, wt_ref, wcol_ref, sin_ref, send_ref,
    tail, state, scale, ewend, offset, cw_ref, cb_ref,
):
    step = pl.program_id(0)
    heads = step_ref.shape[0]
    inner = xs_ref.shape[0]
    width = inner // heads
    taps = cw_ref.shape[0]
    n_state = bc_ref.shape[0] // 2

    @pl.when(step == 0)
    def _():
        for k in range(taps):
            spread_lanes(chan_ref, k, cw_ref.at[k])
        spread_lanes(chan_ref, taps, cb_ref)
        for k in range(taps - 1):
            tail[k] = pltpu.roll(halo_ref[...].astype(F32), taps - 1 - k, 1)
        state[...] = jnp.zeros_like(state)
        offset[...] = jnp.zeros_like(offset)

    dt = softplus(step_ref[...].astype(F32) + bias_ref[...])
    loga = dt * rate_ref[...]
    w = contract(loga, ordered().astype(F32), 1, 0, HIGHEST)
    wcol_ref[...] = contract(ordered(True).astype(F32), loga, 1, 1, HIGHEST)
    wend = jnp.broadcast_to(w[:, BLOCK - 1 :], w.shape)
    dt_ref[...] = dt
    w_ref[...] = w
    wt_ref[...] = w + offset[...]
    offset[...] += wend
    scale[...] = dt * jnp.exp(wend - w)
    ewend[...] = jnp.exp(wend)

    def conv(rows):
        u = u_ref[rows, :].astype(F32)
        lane = lax.broadcasted_iota(jnp.int32, (1, BLOCK), 1)
        c = cb_ref[rows, :] + cw_ref[taps - 1, rows, :] * u
        for k in range(taps - 1):
            back = taps - 1 - k
            rolled = pltpu.roll(u, back, 1)
            c = c + cw_ref[k, rows, :] * jnp.where(lane >= back, rolled, tail[k, rows, :])
            tail[k, rows, :] = rolled
        sig = sigmoid(c)
        value = c * sig
        slope_ref[rows, :] = (sig + value * (1.0 - sig)).astype(LOW)
        return value

    for i in range(2):
        bc_ref[i * n_state : (i + 1) * n_state, :] = conv(
            pl.ds(inner + i * n_state, n_state)
        ).astype(LOW)

    def group(first, rows, parts):
        xs = conv(rows)
        xs_ref[rows, :] = xs.astype(LOW)
        xd = jnp.concatenate([xs[own, :] * scale[h, :] for h, own in parts], axis=0).astype(LOW)
        fresh = contract(xd, bc_ref[:n_state, :], 1, 1)
        old = state[rows, :]
        sin_ref[0, rows, :] = old.astype(LOW)
        state[rows, :] = jnp.concatenate(
            [ewend[h, :] * old[own, :] + fresh[own, :] for h, own in parts], axis=0
        )

    grouped(heads, width, group)

    @pl.when(step == pl.num_programs(0) - 1)
    def _():
        send_ref[:inner, :] = state[...].astype(LOW)
        send_ref[inner:, :] = jnp.exp(offset[...]).astype(LOW)


def scan_states(u, chan, taps, bias, rate, heads, n_state):
    channels = chan.shape[0]
    length = u.shape[1] - BLOCK
    inner = channels - 2 * n_state
    blocks = length // BLOCK
    return call(
        states_kernel,
        (blocks,),
        [
            tokens(u, lambda b: b, channels),
            tokens(u, lambda b: blocks, channels),
            tokens(u, lambda b: b, heads, channels // heads),
            whole(chan), whole(bias), whole(rate),
        ],
        [
            token_out(inner, length, LOW),
            token_out(channels, length, LOW),
            token_out(2 * n_state, length, LOW),
            token_out(heads, length, F32),
            token_out(heads, length, F32),
            token_out(heads, length, F32),
            (out((length, heads), F32), pl.BlockSpec((BLOCK, heads), lambda b: (b, 0))),
            (
                out((blocks, inner, n_state), LOW),
                pl.BlockSpec((1, inner, n_state), lambda b: (b, 0, 0)),
            ),
            fixed_out((inner + heads, n_state), LOW),
        ],
        [
            pltpu.VMEM((taps - 1, channels, BLOCK), F32),
            pltpu.VMEM((inner, n_state), F32),
            pltpu.VMEM((heads, BLOCK), F32),
            pltpu.VMEM((heads, BLOCK), F32),
            pltpu.VMEM((heads, BLOCK), F32),
            pltpu.VMEM((taps, channels, BLOCK), F32),
            pltpu.VMEM((channels, BLOCK), F32),
        ],
        2 * length * inner * n_state,
        channels * length * 8,
        channels * length,
    )


def spread_columns(wcol_ref, wb):
    for h in range(wb.shape[0]):
        wb[h] = jnp.broadcast_to(wcol_ref[:, h : h + 1] * LOG2E, (BLOCK, BLOCK))


def masked_scores(bc_ref, n_state):
    scores = contract(bc_ref[:n_state, :], bc_ref[n_state:, :], 0, 0)
    return jnp.where(ordered(), scores, 0.0)


def decay(wrow, wb_h):
    return jnp.exp2(jnp.minimum(wrow * LOG2E - wb_h, 0.0))


def local_kernel(xs_ref, bc_ref, dt_ref, w_ref, wcol_ref, sin_ref, y_ref, wb, scores):
    heads = dt_ref.shape[0]
    inner = xs_ref.shape[0]
    width = inner // heads
    n_state = bc_ref.shape[0] // 2
    spread_columns(wcol_ref, wb)
    scores[...] = masked_scores(bc_ref, n_state)

    def group(first, rows, parts):
        entering = contract(sin_ref[0, rows, :], bc_ref[n_state:, :], 1, 0)
        xs = xs_ref[rows, :].astype(F32)
        result = []
        for i, (h, own) in enumerate(parts):
            wrow = w_ref[h, :]
            xdt = (xs[own, :] * dt_ref[h, :]).astype(LOW)
            weights = (scores[...] * decay(wrow, wb[first + i])).astype(LOW)
            result.append(entering[own, :] * jnp.exp(wrow) + contract(xdt, weights, 1, 0))
        y_ref[rows, :] = jnp.concatenate(result, axis=0).astype(y_ref.dtype)

    grouped(heads, width, group)


def scan_local(xs, bc, dt, w, wcol, sin):
    inner, length = xs.shape
    heads = dt.shape[0]
    return call(
        local_kernel,
        (length // BLOCK,),
        [
            tokens(xs),
            tokens(bc),
            tokens(dt),
            tokens(w),
            (wcol, pl.BlockSpec((BLOCK, heads), lambda b: (b, 0))),
            (sin, pl.BlockSpec((1,) + sin.shape[1:], lambda b: (b, 0, 0))),
        ],
        [token_out(inner, length, LOW)],
        [pltpu.VMEM((heads, BLOCK, BLOCK), F32), pltpu.VMEM((BLOCK, BLOCK), F32)],
        2 * length * inner * (BLOCK * 4 + bc.shape[0] // 2),
        inner * length * 6,
        heads * length * BLOCK,
    )[0]


def gate_kernel(
    yl_ref, xs_ref, z_ref, bc_ref, wt_ref, sdev_ref, skip_ref, gain_ref,
    ylow_ref, halves_ref, gated_ref, v_scr, total, *, order,
):
    inner = yl_ref.shape[0]
    heads = wt_ref.shape[0]
    width = inner // heads
    half = width // 2
    n_state = bc_ref.shape[0] // 2
    total[...] = jnp.zeros_like(total)

    def group(first, rows, parts):
        corr = contract(sdev_ref[rows, :], bc_ref[n_state:, :], 1, 0)
        xs = xs_ref[rows, :].astype(F32)
        extra = jnp.concatenate(
            [jnp.exp(wt_ref[h, :]) * corr[own, :] + skip_ref[h, :] * xs[own, :] for h, own in parts],
            axis=0,
        )
        y = (yl_ref[rows, :].astype(F32) + extra).astype(LOW)
        ylow_ref[rows, :] = y
        z = z_ref[rows, :].astype(F32)
        v = y.astype(F32) * (z * sigmoid(z))
        v_scr[rows, :] = v
        total[...] += fold(v * v)

    grouped(heads, width, group)
    r = lax.rsqrt(column_sum(total[...]) / inner + EPSILON)
    for h in range(heads):
        rows = slice(h * width, (h + 1) * width)
        gated = (v_scr[rows, :] * r * gain_ref[rows, :]).astype(LOW)
        for c in range(2):
            piece = gated[c * half : (c + 1) * half, :]
            halves_ref[c, h * half : (h + 1) * half, :] = piece
            if order is None:
                gated_ref[h * width + c * half : h * width + (c + 1) * half, :] = piece
            else:
                at = order[h][1] * half
                gated_ref[order[h][0], c, at : at + half, :] = piece


def gate_forward(yl, xs, z, bc, wt, sdev, skip, gain, order):
    inner, length = yl.shape
    heads = wt.shape[0]
    if order is None:
        gated = token_out(inner, length, LOW)
    else:
        shape = (2, 2, inner // 4)
        gated = (
            out(shape + (length,), LOW), pl.BlockSpec(shape + (BLOCK,), lambda b: (0, 0, 0, b))
        )
    pair = (2, inner // 2)
    halves = (out(pair + (length,), LOW), pl.BlockSpec(pair + (BLOCK,), lambda b: (0, 0, b)))
    return call(
        functools.partial(gate_kernel, order=order),
        (length // BLOCK,),
        [
            tokens(yl), tokens(xs), tokens(z), tokens(bc), tokens(wt), whole(sdev), whole(skip), whole(gain),
        ],
        [token_out(inner, length, LOW), halves, gated],
        [
            pltpu.VMEM((inner, BLOCK), F32),
            pltpu.VMEM((8, BLOCK), F32),
        ],
        2 * length * inner * sdev.shape[1],
        inner * length * 14,
        inner * length,
    )


def gate_back_kernel(
    dg0_ref, dg1_ref, ylow_ref, z_ref, bc_ref, wt_ref, gain_ref, decays_ref,
    dy_ref, dz_ref, gsum_ref, send_ref, ds, gg, sums, sig_scr, dg_ref,
):
    step = pl.program_id(0)
    inner = ylow_ref.shape[0]
    heads = wt_ref.shape[0]
    width = inner // heads
    n_state = bc_ref.shape[0] // 2

    @pl.when(step == 0)
    def _():
        gg[...] = jnp.zeros_like(gg)
        ds[...] = jnp.zeros_like(ds)

    sums[...] = jnp.zeros_like(sums)
    half = width // 2

    def first_pass(first, rows, parts):
        own = pl.ds(pl.multiple_of(first * half, len(parts) * half), len(parts) * half)
        both = [ref[own, :].astype(F32) for ref in (dg0_ref, dg1_ref)]
        dg_ref[rows, :] = jnp.concatenate(
            [both[c][i * half : (i + 1) * half, :] for i in range(len(parts)) for c in range(2)], axis=0
        )
        z = z_ref[rows, :].astype(F32)
        sig = sigmoid(z)
        sig_scr[rows, :] = sig
        v = ylow_ref[rows, :].astype(F32) * (z * sig)
        m = v * (dg_ref[rows, :] * gain_ref[rows, :])
        sums[0] += fold(v * v)
        sums[1] += fold(m)

    grouped(heads, width, first_pass)
    r = lax.rsqrt(column_sum(sums[0]) / inner + EPSILON)
    back = r * r * r * (column_sum(sums[1]) / inner)

    def second_pass(first, rows, parts):
        z = z_ref[rows, :].astype(F32)
        sig = sig_scr[rows, :]
        silu = z * sig
        y = ylow_ref[rows, :].astype(F32)
        v = y * silu
        du = dg_ref[rows, :]
        dv = r * (gain_ref[rows, :] * du) - v * back
        dy = (dv * silu).astype(LOW)
        dy_ref[rows, :] = dy
        dz_ref[rows, :] = (dv * y * (sig + silu * (1.0 - sig))).astype(LOW)
        gg[rows, :] += du * v * r
        dy = dy.astype(F32)
        dye = jnp.concatenate([dy[own, :] * jnp.exp(wt_ref[h, :]) for h, own in parts], axis=0)
        ds[rows, :] += contract(dye.astype(LOW), bc_ref[n_state:, :], 1, 1)

    grouped(heads, width, second_pass)

    @pl.when(step == pl.num_programs(0) - 1)
    def _():
        send_ref[:inner, :] = ds[...].astype(LOW)
        send_ref[inner:, :] = decays_ref[...]
        for at in range(0, inner, BLOCK):
            rows = slice(at, at + BLOCK)
            gsum_ref[0:1, rows] = column_sum(gg[rows, :].T)


def gate_backward(dg0, dg1, ylow, z, bc, wt, gain, decays):
    inner, length = ylow.shape
    heads = wt.shape[0]
    n_state = bc.shape[0] // 2
    return call(
        gate_back_kernel,
        (length // BLOCK,),
        [
            tokens(dg0), tokens(dg1),
            tokens(ylow), tokens(z), tokens(bc), tokens(wt), whole(gain), whole(decays),
        ],
        [
            token_out(inner, length, LOW),
            token_out(inner, length, LOW),
            fixed_out((8, inner), F32),
            fixed_out((inner + heads, n_state), LOW),
        ],
        [
            pltpu.VMEM((inner, n_state), F32),
            pltpu.VMEM((inner, BLOCK), F32),
            pltpu.VMEM((2, 8, BLOCK), F32),
            pltpu.VMEM((inner, BLOCK), F32),
            pltpu.VMEM((inner, BLOCK), F32),
        ],
        0,
        0,
    )


def local_back_kernel(
    xs_ref, dy_ref, bc_ref, dt_ref, w_ref, wcol_ref, dx_ref, rows_ref, dbc_ref, wb, scores, dscores
):
    heads = dt_ref.shape[0]
    inner = xs_ref.shape[0]
    width = inner // heads
    n_state = bc_ref.shape[0] // 2
    spread_columns(wcol_ref, wb)
    scores[...] = masked_scores(bc_ref, n_state)
    dscores[...] = jnp.zeros_like(dscores)

    def group(first, rows, parts):
        xs = xs_ref[rows, :].astype(F32)
        dy_all = dy_ref[rows, :]
        result, total = [], 0.0
        for i, (h, own) in enumerate(parts):
            xdt = (xs[own, :] * dt_ref[h, :]).astype(LOW)
            dy = dy_all[own, :]
            decays = decay(w_ref[h, :], wb[first + i])
            weights = (scores[...] * decays).astype(LOW)
            y = contract(xdt, weights, 1, 0)
            dx = contract(dy, weights, 1, 1)
            total = total + decays * contract(xdt, dy, 0, 0)
            result.append(dx)
            rows_ref[h, :] = column_sum(dy.astype(F32) * y - xdt.astype(F32) * dx)
        dscores[...] += total
        dx_ref[rows, :] = jnp.concatenate(result, axis=0).astype(dx_ref.dtype)

    grouped(heads, width, group)
    masked = jnp.where(ordered(), dscores[...], 0.0).astype(LOW)
    dbc_ref[:n_state, :] = contract(bc_ref[n_state:, :], masked, 1, 1)
    dbc_ref[n_state:, :] = contract(bc_ref[:n_state, :], masked, 1, 0)


def scan_local_back(xs, dy, bc, dt, w, wcol):
    inner, length = xs.shape
    heads = dt.shape[0]
    return call(
        local_back_kernel,
        (length // BLOCK,),
        [
            tokens(xs),
            tokens(dy),
            tokens(bc),
            tokens(dt),
            tokens(w),
            (wcol, pl.BlockSpec((BLOCK, heads), lambda b: (b, 0))),
        ],
        [
            token_out(inner, length, LOW),
            token_out(heads, length, F32),
            token_out(bc.shape[0], length, F32),
        ],
        [
            pltpu.VMEM((heads, BLOCK, BLOCK), F32),
            pltpu.VMEM((BLOCK, BLOCK), F32),
            pltpu.VMEM((BLOCK, BLOCK), F32),
        ],
        2 * length * inner * BLOCK * 12,
        inner * length * 6,
        heads * length * BLOCK,
    )


def states_back_kernel(
    u_ref, halo_ref, step_ref, slope_ref, xs_ref, dy_ref, dxl_ref, dbcl_ref, bc_ref,
    dt_ref, w_ref, wt_ref, rows_ref, sin_ref, sdev_ref, dsend_ref,
    chan_ref, bias_ref, rate_ref, skip_ref,
    du_ref, first_ref, csum_ref, hsum_ref,
    ds, toend, ew, ewend, offs, rr, kk, ddt, ee, right, gconv, ghead, dbc, dc_first, cw_ref,
):
    step = pl.program_id(0)
    final = pl.num_programs(0) - 1
    heads = step_ref.shape[0]
    inner = xs_ref.shape[0]
    channels = u_ref.shape[0]
    width = inner // heads
    n_state = bc_ref.shape[0] // 2
    taps = cw_ref.shape[0]
    subs = sin_ref.shape[0]
    spans = [slice(s * BLOCK, (s + 1) * BLOCK) for s in range(subs)]
    backwards = list(reversed(range(subs)))

    @pl.when(step == 0)
    def _():
        ds[...] = dsend_ref[...]
        for k in range(taps):
            spread_lanes(chan_ref, k, cw_ref.at[k])
        right[...] = jnp.zeros_like(right)
        gconv[...] = jnp.zeros_like(gconv)
        ghead[...] = jnp.zeros_like(ghead)

    for s in range(subs):
        w = w_ref[:, spans[s]]
        wend = jnp.broadcast_to(w[:, BLOCK - 1 :], w.shape)
        toend[s] = jnp.exp(wend - w)
        ew[s] = jnp.exp(w)
        ewend[s] = jnp.exp(wend)
        offs[s] = jnp.exp(wt_ref[:, spans[s]] - w)
        dbc[s] = dbcl_ref[:, spans[s]]

    def conv_back(rows, dxs):
        lane = lax.broadcasted_iota(jnp.int32, (1, BLOCK), 1)
        carried = [right[k, rows, :] for k in range(taps - 1)]
        sums = [gconv[k, rows, :] for k in range(taps + 1)]
        for s in backwards:
            u = u_ref[rows, spans[s]].astype(F32)
            dc = dxs[s] * slope_ref[rows, spans[s]].astype(F32)
            du = cw_ref[taps - 1, rows, :] * dc
            sums[taps - 1] = sums[taps - 1] + u * dc
            sums[taps] = sums[taps] + dc
            for k in range(taps - 1):
                ahead = taps - 1 - k
                rolled = pltpu.roll(dc, BLOCK - ahead, 1)
                moved = jnp.where(lane < BLOCK - ahead, rolled, carried[k])
                carried[k] = rolled
                du = du + cw_ref[k, rows, :] * moved
                sums[k] = sums[k] + u * moved
            du_ref[rows, spans[s]] = du.astype(LOW)
        for k in range(taps - 1):
            right[k, rows, :] = carried[k]
        for k in range(taps + 1):
            gconv[k, rows, :] = sums[k]
        dc_first[rows, :] = dc

    def group(first, rows, parts):
        sdev = sdev_ref[rows, :].astype(F32)
        d = ds[rows, :]
        b_low = bc_ref[:n_state, :]
        c_low = bc_ref[n_state:, :]
        all_dxs = [None] * subs
        for s in backwards:
            sin = sin_ref[s, rows, :].astype(F32)
            entering = jnp.concatenate(
                [sin[own, :] + offs[s, h, :] * sdev[own, :] for h, own in parts], axis=0
            )
            cross = d * entering
            for h, own in parts:
                ee[s, h, :] = ewend[s, h, :] * column_sum(cross[own, :])
            d_low = d.astype(LOW)
            entering_low = entering.astype(LOW)
            q = contract(d_low, b_low[:, spans[s]], 1, 0)
            yo = contract(entering_low, c_low[:, spans[s]], 1, 0)
            xs = xs_ref[rows, spans[s]].astype(F32)
            dy = dy_ref[rows, spans[s]].astype(F32)
            dxl = dxl_ref[rows, spans[s]].astype(F32)
            xde, dye, dxs = [], [], []
            for h, own in parts:
                te, eh, dt = toend[s, h, :], ew[s, h, :], dt_ref[h, spans[s]]
                x, g = xs[own, :], dy[own, :]
                xe = x * dt * te
                ge = g * eh
                kk[s, h, :] = column_sum(xe * q[own, :])
                rr[s, h, :] = rows_ref[h, spans[s]] + column_sum(ge * yo[own, :])
                xde.append(xe)
                dye.append(ge)
                dx = dxl[own, :] + te * q[own, :]
                ddt[s, h, :] = column_sum(dx * x)
                ghead[2, h, :] += column_sum(g * x)
                dxs.append(dx * dt + skip_ref[h, :] * g)
            xde = jnp.concatenate(xde, axis=0).astype(LOW)
            dye = jnp.concatenate(dye, axis=0).astype(LOW)
            dbc[s, :n_state, :] += contract(d_low, xde, 0, 0)
            dbc[s, n_state:, :] += contract(entering_low, dye, 0, 0)
            fresh = contract(dye, c_low[:, spans[s]], 1, 1)
            d = jnp.concatenate(
                [ewend[s, h, :] * d[own, :] + fresh[own, :] for h, own in parts], axis=0
            )
            all_dxs[s] = jnp.concatenate(dxs, axis=0)
        ds[rows, :] = d
        conv_back(rows, all_dxs)

    grouped(heads, width, group)
    for i in range(2):
        at = slice(i * n_state, (i + 1) * n_state)
        conv_back(pl.ds(inner + i * n_state, n_state), [dbc[s, at, :] for s in range(subs)])

    upper = ordered().astype(F32)
    rate = rate_ref[...]
    for s in range(subs):
        dloga = (
            contract(rr[s], upper, 1, 1, HIGHEST)
            + (contract(kk[s], upper, 1, 0, HIGHEST) - kk[s])
            + jnp.sum(ee[s], axis=1, keepdims=True)
        )
        dt = dt_ref[:, spans[s]]
        raw = step_ref[:, spans[s]].astype(F32) + bias_ref[...]
        dstep = (ddt[s] + dloga * rate) * sigmoid(raw)
        du_ref[channels:, spans[s]] = dstep.astype(LOW)
        ghead[0] += dstep
        ghead[1] += dloga * dt * rate

    @pl.when(step == final)
    def _():
        first_ref[...] = dc_first[...].T[: first_ref.shape[0], :]
        lane = lax.broadcasted_iota(jnp.int32, (1, BLOCK), 1)
        for at in range(0, channels, BLOCK):
            rows = slice(at, at + BLOCK)
            halo = halo_ref[rows, :].astype(F32)
            dc = dc_first[rows, :]
            for k in range(taps + 1):
                total = gconv[k, rows, :]
                if k < taps - 1:
                    back = taps - 1 - k
                    total = total + jnp.where(lane < back, pltpu.roll(halo, back, 1) * dc, 0.0)
                csum_ref[k : k + 1, rows] = column_sum(total.T)
        for i in range(3):
            hsum_ref[:, i : i + 1] = jnp.sum(ghead[i], axis=1, keepdims=True)


def scan_states_back(
    u, slope, xs, dy, dx_local, dbc_local, bc, dt, w, wt, row_sums, sin, sdev, dsend,
    chan, taps, bias, rate, skip,
):
    channels, length = slope.shape
    heads = dt.shape[0]
    inner = xs.shape[0]
    steps = length // (SUBS * BLOCK)
    n_state = bc.shape[0] // 2
    span = SUBS * BLOCK
    place = lambda b: steps - 1 - b

    def pairs(array, rows=None, at=0):
        rows = array.shape[0] if rows is None else rows
        return (array, pl.BlockSpec((rows, span), lambda b: (at, place(b))))

    def pairs_out(rows, dtype):
        return (out((rows, length), dtype), pl.BlockSpec((rows, span), lambda b: (0, place(b))))

    per_head = pltpu.VMEM((SUBS, heads, BLOCK), F32)
    return call(
        states_back_kernel,
        (steps,),
        [
            pairs(u, channels),
            tokens(u, lambda b: length // BLOCK, channels),
            pairs(u, heads, channels // heads),
            pairs(slope),
            pairs(xs),
            pairs(dy),
            pairs(dx_local),
            pairs(dbc_local),
            pairs(bc),
            pairs(dt),
            pairs(w),
            pairs(wt),
            pairs(row_sums),
            (sin, pl.BlockSpec((SUBS,) + sin.shape[1:], lambda b: (place(b), 0, 0))),
            whole(sdev),
            whole(dsend),
            whole(chan),
            whole(bias),
            whole(rate),
            whole(skip),
        ],
        [
            pairs_out(channels + heads, LOW),
            fixed_out((8, channels), F32),
            fixed_out((8, channels), F32),
            fixed_out((heads, 8), F32),
        ],
        [
            pltpu.VMEM((inner, n_state), F32),
            per_head,
            per_head,
            per_head,
            per_head,
            per_head,
            per_head,
            per_head,
            per_head,
            pltpu.VMEM((taps - 1, channels, BLOCK), F32),
            pltpu.VMEM((taps + 1, channels, BLOCK), F32),
            pltpu.VMEM((3, heads, BLOCK), F32),
            pltpu.VMEM((SUBS, 2 * n_state, BLOCK), F32),
            pltpu.VMEM((channels, BLOCK), F32),
            pltpu.VMEM((taps, channels, BLOCK), F32),
        ],
        2 * length * inner * n_state * 5,
        inner * length * 14 + taps * channels * 1024,
        channels * length,
    )


def edge_kernel(du_ref, ahead_ref, chan_ref, out_ref, *, taps):
    lanes = du_ref.shape[1]
    channels = ahead_ref.shape[1]
    lane = lax.broadcasted_iota(jnp.int32, (1, lanes), 1)
    for at in range(0, channels, lanes):
        rows = slice(at, at + lanes)
        ahead = jnp.concatenate(
            [ahead_ref[:, rows], jnp.zeros((lanes - ahead_ref.shape[0], lanes), F32)], axis=0
        ).T
        du = du_ref[rows, :].astype(F32)
        for k in range(taps - 1):
            back = taps - 1 - k
            moved = pltpu.roll(ahead, lanes - back, 1)
            du = du + jnp.where(lane >= lanes - back, chan_ref[rows, k : k + 1] * moved, 0.0)
        out_ref[rows, :] = du.astype(LOW)


def add_edge(du, ahead, chan, taps):
    channels = ahead.shape[1]
    last = du.shape[1] // BLOCK - 1
    block = pl.BlockSpec((channels, BLOCK), lambda b: (0, last))
    return pl.pallas_call(
        functools.partial(edge_kernel, taps=taps),
        grid=(1,),
        in_specs=[block, whole(ahead)[1], whole(chan)[1]],
        out_specs=block,
        out_shape=out(du.shape, LOW),
        input_output_aliases={0: 0},
        compiler_params=pltpu.CompilerParams(vmem_limit_bytes=VMEM_BYTES),
        cost_estimate=pl.CostEstimate(flops=0, bytes_accessed=channels * 3000, transcendentals=0),
    )(du, ahead, chan)


def shifted(x, axis, by):
    devices = lax.axis_size(axis)
    return lax.ppermute(
        x, axis, [(i, i + by) for i in range(devices) if 0 <= i + by < devices]
    )


def swapped(x):
    return lax.ppermute(x, "section", [(0, 1), (1, 0)])


def after(value, *others):
    return lax.optimization_barrier((value,) + others)[0]


def summed(value, axes):
    for axis in axes:
        reach = 1
        while reach < lax.axis_size(axis):
            pairs = [(i, i ^ reach) for i in range(lax.axis_size(axis))]
            value = value + lax.ppermute(value, axis, pairs)
            reach *= 2
    return value


def chained(own, inner, heads, toward, beside):
    devices = lax.axis_size("head")
    shape = (heads, inner // heads, own.shape[1])
    split = lambda a: (a[:inner].astype(F32).reshape(shape), a[inner:].astype(F32)[:, :1, None])
    if devices <= 4:
        got = [shifted(own, "head", toward * k) for k in range(1, devices)]
        terms = [split(a) for a in lax.optimization_barrier((*got, beside))[:-1]]
        total = terms[-1][0]
        for state, factor in terms[-2::-1]:
            total = state + factor * total
        return total.reshape(inner, own.shape[1])
    index = lax.axis_index("head")
    everyone = lax.all_gather(own, "head", axis=0)
    total = jnp.zeros(shape, F32)
    for m in range(devices) if toward == 1 else range(devices - 1, -1, -1):
        state, factor = split(everyone[m])
        before = (m < index) if toward == 1 else (m > index)
        total = jnp.where(before, total * factor + state, total)
    return total.reshape(inner, own.shape[1])


def gathered(in_shard, out_shard, joined):
    section = lax.axis_index("section")
    layers = lax.axis_size("section")
    rows = in_shard.shape[0]
    model = out_shard.shape[1]
    across = ("seq", "head", "section")
    halves = lambda a: a.reshape((2, a.shape[0] // 2) + a.shape[1:])

    def pieces(a):
        a = halves(a)
        own = lax.dynamic_index_in_dim(a, section, 0, keepdims=False)
        got = swapped(lax.dynamic_index_in_dim(a, 1 - section, 0, keepdims=False))
        return [jnp.where(section == i, own, got) for i in range(layers)]

    everyone = lambda a: lax.all_gather(a, across, axis=0, tiled=True)
    result = []
    if joined:
        side = out_shard.reshape(2, 2, rows // 2, model).transpose(0, 2, 1, 3).reshape(rows, 2 * model)
        first, *others = pieces(jnp.concatenate([side, in_shard], axis=1))
        every = everyone(first)
        result.append((lambda since: every[:, : 2 * model], every[:, 2 * model :]))
        for piece in others:
            w_in = everyone(piece[:, 2 * model :])
            result.append(
                (lambda since, piece=piece: everyone(after(piece[:, : 2 * model], since)), w_in)
            )
        return result
    for in_piece, out_piece in zip(pieces(in_shard), pieces(out_shard)):
        w_in = everyone(in_piece)
        result.append((lambda since, out_piece=out_piece: everyone(out_piece), w_in))
    return result


def products(left, rights, index):
    return jnp.concatenate(
        [
            contract(lax.dynamic_index_in_dim(a, index, 0, keepdims=False), b, 1, dim)
            for a, (b, dim) in zip(left, rights)
        ],
        axis=1,
    )


def pair_sent(left, rights):
    return products(left, rights, 1 - lax.axis_index("section")).astype(LOW)


def pair_sum(left, rights, sent):
    own = products(left, rights, lax.axis_index("section"))
    return (own + swapped(sent).astype(F32)).astype(LOW)


def over_head(part, beside=()):
    count = lax.axis_size("head")
    rows, columns = part.shape
    part = after(lax.all_to_all(part, "head", split_axis=0, concat_axis=0, tiled=True), *beside)
    return jnp.sum(part.reshape(count, rows // count, columns).astype(F32), axis=0).astype(LOW)


def over_seq(part, beside=()):
    count = lax.axis_size("seq")
    rows, columns = part.shape
    part = after(lax.all_to_all(part, "seq", split_axis=0, concat_axis=0, tiled=True), *beside)
    return jnp.sum(part.reshape(count, rows // count, columns).astype(F32), axis=0)


def over_both(part):
    return lax.psum_scatter(part, ("head", "seq"), scatter_dimension=0, tiled=True).astype(F32)


def by_owner(values, split):
    seqs, heads_n = lax.axis_size("seq"), lax.axis_size("head")
    rows, columns = values.shape
    own = rows // (seqs * heads_n * 2 * split)
    values = values.reshape(seqs, heads_n, 2, split, own, columns)
    return values.transpose(2, 3, 1, 0, 4, 5).reshape(2, split, seqs * heads_n * own, columns)


def rms_inverse(h):
    return lax.rsqrt(jnp.mean(h * h, axis=-1, keepdims=True) + EPSILON)


def spread(values):
    return jnp.broadcast_to(values[..., None], values.shape + (BLOCK,))


def columns(*vectors):
    rows = [v[None] for v in vectors]
    rows.append(jnp.zeros((8 - len(vectors), vectors[0].shape[0]), F32))
    return jnp.concatenate(rows, axis=0).T


def first_norm(h, p):
    normed = (h * rms_inverse(h) * p["norm_gain"]).astype(LOW)
    edge = shifted(after(h[-8:], *p["early"]), "head", 1)
    edge = (edge * rms_inverse(edge) * p["norm_gain"]).astype(LOW)
    padded = jnp.concatenate([normed, jnp.zeros((BLOCK - 8, h.shape[1]), LOW), edge], axis=0)
    return normed, padded


def layer_forward(h, normed, padded, p):
    inner, n_state, heads = p["inner"], p["n_state"], p["heads"]
    u = contract(p["w_x"], padded, 0, 1).astype(LOW)
    z = contract(p["w_z"], normed, 0, 1).astype(LOW)
    xs, slope, bc, dt, w, wt, wcol, sin, send = scan_states(
        u, p["chan"], p["taps"], p["bias"], p["rate"], heads, n_state
    )
    y_local = scan_local(xs, bc, dt, w, wcol, sin)
    sdev = chained(send, inner, heads, 1, y_local).astype(LOW)
    ylow, halves, gated = gate_forward(
        y_local, xs, z, bc, wt, sdev, p["skip"], p["gate_gain"], p["order"]
    )
    if p["order"] is None:
        gated = by_owner(gated, 2)
    result = h + contract(halves[0], p["w_o"][0], 0, 0) + contract(halves[1], p["w_o"][1], 0, 0)
    kept = dict(
        h=h, normed_rows=by_owner(normed.T, 1)[:, 0], z=z, u=u, slope=slope, xs=xs, bc=bc, dt=dt, w=w, wt=wt,
        wcol=wcol, sin=sin, sdev=sdev, ylow=ylow, gated=gated, decays=send[inner:],
    )
    return result, kept


def layer_backward(g, p, k, finished, pending):
    inner, n_state, heads, last, taps = p["inner"], p["n_state"], p["heads"], p["last"], p["taps"]
    g_low = after(g.astype(LOW), *finished)
    dg = [contract(w, g_low, 1, 1).astype(LOW) for w in p["w_o"]]
    if last:
        pending = over_head(pending)
    normed_rows = k["normed_rows"]
    dy, dz, gsum, send = gate_backward(
        dg[0], dg[1], k["ylow"], k["z"], k["bc"], k["wt"], p["gate_gain"], k["decays"]
    )
    left = [k["gated"][:, 0], k["gated"][:, 1], normed_rows]
    rights = [(g_low, 0), (g_low, 0), (dz, 1)]
    sent = pair_sent(left, rights)
    if last:
        sent = after(sent, pending)
    dx_local, row_sums, dbc_local = scan_local_back(
        k["xs"], after(dy, sent), k["bc"], k["dt"], k["w"], k["wcol"]
    )
    if last:
        pending = over_seq(pending, (dx_local,))
    dsend = chained(send, inner, heads, -1, dx_local)
    early = pair_sum(left, rights, sent)
    du, first, csum, hsum = scan_states_back(
        k["u"], k["slope"], k["xs"], dy, after(dx_local, early), dbc_local, k["bc"], k["dt"], k["w"],
        k["wt"], row_sums, k["sin"], k["sdev"], dsend, p["chan"], p["taps"], p["bias"], p["rate"], p["skip"],
    )
    ahead = shifted(first, "head", -1)
    dnormed = contract(after(dz, first), p["w_z"], 0, 1)
    if last:
        early = over_head(after(early, dsend, dx_local, pending), (dnormed,))
        du = after(du, early, dnormed)
        early = over_seq(early)
    else:
        early = over_both(early)
        du = after(du, dnormed)
    du = add_edge(du, ahead, p["chan"], taps)
    left, rights = [normed_rows], [(du, 1)]
    sent = pair_sent(left, rights)
    late = pair_sum(left, rights, after(sent, early) if last else sent)
    dnormed = dnormed + contract(after(du, late), p["w_x"], 0, 1)
    h = k["h"]
    r = rms_inverse(h)
    wd = dnormed * p["norm_gain"]
    dh = r * wd - h * (r * r * r * jnp.mean(wd * h, axis=-1, keepdims=True))
    small = jnp.concatenate(
        [
            jnp.sum(dnormed * h * r, axis=0),
            csum[: taps + 1].reshape(-1),
            hsum[:, :3].T.reshape(-1),
            gsum[0],
        ]
    )
    return g + dh, early, late, pending, small


def local(
    section_ends, norm_gain, in_weight, conv_weight, conv_bias, dt_bias, a_log, skip_gain, gated_gain, out_weight,
):
    section = lax.axis_index("section")
    layers = lax.axis_size("section")
    seqs, heads_n = lax.axis_size("seq"), lax.axis_size("head")
    inner = gated_gain.shape[1]
    heads = dt_bias.shape[1]
    width = inner // heads
    n_state = (conv_bias.shape[1] - inner) // 2
    model = norm_gain.shape[1]
    ends = section_ends[0, :, 0]
    turned = jnp.where(section == 0, ends[1], ends[0])
    received = swapped(turned)
    hidden = jnp.where(section == 0, ends[0], received)
    cotangent = jnp.where(section == 0, received, ends[1])

    joined = out_weight.shape[1] == 2 * width and in_weight.shape[1] == width
    weights = gathered(in_weight[0].astype(LOW), out_weight[0].astype(LOW), joined)
    mine = (norm_gain, conv_weight, conv_bias, dt_bias, a_log, skip_gain, gated_gain)
    flat = jnp.concatenate([a.reshape(-1) for a in mine])
    other = swapped(flat)
    params = []
    for i in range(layers):
        own = jnp.where(section == i, flat, other)
        parts, at = [], 0
        for a in mine:
            parts.append(own[at : at + a.size].reshape(a.shape[1:]))
            at += a.size
        gain, cw, cb, bias, alog, skip, gate_gain = parts
        w_out, w_in = weights[i]
        order = tuple((h % 2, (h // 2 % heads_n) * seqs + h // 2 // heads_n) for h in range(heads))
        params.append(
            dict(
                inner=inner,
                n_state=n_state,
                heads=heads,
                order=order if joined else None,
                last=i == 0,
                norm_gain=gain,
                w_z=w_in[:, :inner],
                w_x=w_in[:, inner:],
                w_out=w_out,
                taps=cw.shape[0],
                chan=columns(*cw, cb),
                bias=spread(bias),
                rate=spread(-jnp.exp(alog)),
                skip=spread(skip),
                gate_gain=spread(gate_gain),
            )
        )

    prepared = [p[name] for p in params for name in ("chan", "bias", "rate", "skip", "gate_gain")]
    params[0]["early"] = prepared
    params[1]["early"] = []
    kept = []
    for p in params:
        normed, padded = first_norm(hidden, p)
        if kept:
            padded = after(padded, kept[-1]["normed_rows"])
        w_out = p["w_out"](kept[-1]["u"] if kept else None)
        if joined:
            p["w_o"] = (w_out[:, :model], w_out[:, model:])
        else:
            w_o = w_out.reshape(heads, 2, width // 2, model).transpose(1, 0, 2, 3)
            p["w_o"] = w_o.reshape(2, inner // 2, model)
        hidden, k = layer_forward(hidden, normed, padded, p)
        kept.append(k)
    hidden_other = lax.ppermute(hidden, "section", [(0, 1)])
    grad = after(cotangent, hidden)
    grad, early_1, late_1, _, small_1 = layer_backward(grad, params[1], kept[1], [], None)
    grad, early_0, late_0, late_1, small_0 = layer_backward(
        grad, params[0], kept[0], [early_1], late_1
    )
    grad_other = lax.ppermute(grad, "section", [(1, 0)])
    first = section == 0
    ends_out = jnp.stack(
        [jnp.where(first, grad, hidden_other), jnp.where(first, grad_other, hidden)]
    )

    total = jnp.where(first, small_0, small_1) + swapped(jnp.where(first, small_1, small_0))
    total = summed(total, ("head", "seq"))
    grads, at = [], 0
    for a in (norm_gain, conv_weight, conv_bias, dt_bias, a_log, skip_gain, gated_gain):
        grads.append(total[at : at + a.size].reshape(a.shape))
        at += a.size
    norm_g, conv_g, shift_g, bias_g, alog_g, skip_g, gate_g = grads
    late_0 = over_seq(over_head(late_0))
    rows = [
        jnp.concatenate([early_0, after(late_0, *grads)], axis=1),
        jnp.concatenate([early_1, late_1], axis=1),
    ]
    got = swapped(jnp.where(first, rows[1], rows[0]))
    own = jnp.where(first, rows[0], rows[1])
    both = jnp.stack([jnp.where(first, own, got), jnp.where(first, got, own)])
    share = both.shape[1]
    out_rows = both[:, :, : 2 * model].reshape(2, share, 2, model).transpose(0, 2, 1, 3)
    out_rows = out_rows.reshape(4 * share, model)
    in_rows = both[:, :, 2 * model :].reshape(2 * share, -1)

    return (
        ends_out[None, :, None], norm_g, in_rows[None], conv_g, shift_g, bias_g, alog_g, skip_g, gate_g,
        out_rows[None],
    )


def solution(mesh):
    in_specs = (
        P("section", None, "seq", "head", None),
        P("section", None),
        P("section", ("seq", "head"), None),
        P("section", None, None),
        P("section", None),
        P("section", None),
        P("section", None),
        P("section", None),
        P("section", None),
        P("section", ("seq", "head"), None),
    )
    return jax.shard_map(local, mesh=mesh, in_specs=in_specs, out_specs=in_specs, check_vma=False)
```
